32 devices in a mesh: tm: 4 (over x, core), space: 8 (over z, y).
Axes of the slice: x: 2, y: 2, z: 4, core: 2. Of those that a mesh axis runs over, the one named last changes fastest.
Arguments:
- source: float32 [4, 128, 256, 128], P('tm', 'space'), may hold values from -24 to 24
- initial: float32 [128, 256, 128], P('space'), may hold values from -24 to 24
- diffusivity: float32 [128, 256, 128], P('space'), may hold values from 0.5 to 6, as said below
Outputs:
- field_steps: float32 [4, 128, 256, 128], P('tm', 'space')
The draws below stay inside these ranges and needn't reach their ends.
Inputs may be any that keep to these rules, and one draw needn't show every extreme that they name: The diffusivity at every cell, positive.
All inputs are finite; a program needn't handle non-finite values.
Results may differ from the reference program's by a relative error of at most 0.0003.
Values sent between devices are 32-bit elements; how exact they have to be, the bound alone decides.
A program may use at most 128 MiB of HBM per device.

```python
import math
import jax
import jax.numpy as jnp

NX = 128
NY = 256
NZ = 128
STEPS = 4


def draw_diffusivity(key, part):
    base = jnp.exp(jax.random.uniform(key, (NX, NY, NZ), jnp.float32, math.log(0.5), math.log(2.0)))
    ramp = 1.0 + 2.0 * jnp.arange(NX, dtype=jnp.float32) / (NX - 1)
    return base * ramp[:, None, None]


def steps_of(stream_key, extent, cuts, smallest, largest):
    level, own = 1.0, jax.random.fold_in(stream_key, 6)
    for position, parts in cuts:
        draws = jnp.exp(jax.random.uniform(jax.random.fold_in(own, position), (parts,), jnp.float32, smallest / len(cuts), largest / len(cuts)))
        level = level * jnp.repeat(draws, extent[position] // parts).reshape([-1 if axis == position else 1 for axis in range(len(extent))])
    return level


def bell_draw(key, shape, width, bound, cuts=(), kind=jnp.bfloat16):
    values = width * jax.random.normal(key, shape, jnp.float32)
    if cuts:
        values = values * steps_of(key, shape, cuts, -0.22, 0.18)
    return jnp.clip(values, -bound, bound).astype(kind)


def setup_inputs(seed: int = 0) -> dict:
    arg_keys = jax.random.split(jax.random.key(seed), 4)
    return {
        "source": bell_draw(arg_keys[0], (STEPS, NX, NY, NZ), 4.0, 24.0, ((0, 4), (1, 8)), jnp.float32),
        "initial": bell_draw(arg_keys[1], (NX, NY, NZ), 4.0, 24.0, ((0, 8),), jnp.float32),
        "diffusivity": draw_diffusivity(jax.random.fold_in(arg_keys[3], 71), 0),
    }


alpha_corner = 0.05
step_length = 1.0

def face_terms(diffusivity):
    listed = []
    for dimension in range(3):
        listed.append(0.5 * (diffusivity + jnp.roll(diffusivity, -1, dimension)))
        listed.append(0.5 * (diffusivity + jnp.roll(diffusivity, 1, dimension)))
    return listed

def diffuse(values, terms):
    accumulated = terms[0] * (values - jnp.roll(values, -1, 0)) + terms[1] * (values - jnp.roll(values, 1, 0))
    accumulated = accumulated + terms[2] * (values - jnp.roll(values, -1, 1)) + terms[3] * (values - jnp.roll(values, 1, 1))
    accumulated = accumulated + terms[4] * (values - jnp.roll(values, -1, 2)) + terms[5] * (values - jnp.roll(values, 1, 2))
    return accumulated

def apply_system(vec_real, vec_imag, terms, shift):
    out_real = shift[0] * vec_real - shift[1] * vec_imag + step_length * diffuse(vec_real, terms)
    out_imag = shift[0] * vec_imag + shift[1] * vec_real + step_length * diffuse(vec_imag, terms)
    return (out_real, out_imag)

def wave_symbol(count, dtype):
    return 4.0 * jnp.sin(math.pi * jnp.arange(count, dtype=dtype) / count) ** 2

def precondition(vec_real, vec_imag, shift, mean_kappa):
    full_x, full_y, full_z = vec_real.shape
    spectrum = jnp.fft.fftn(vec_real + 1j * vec_imag)
    symbol = wave_symbol(full_x, vec_real.dtype)[:, None, None] + wave_symbol(full_y, vec_real.dtype)[None, :, None]
    symbol = symbol + wave_symbol(full_z, vec_real.dtype)[None, None, :]
    denom_real = shift[0] + step_length * mean_kappa * symbol
    denom_imag = shift[1]
    magnitude = denom_real * denom_real + denom_imag * denom_imag
    spec_real = jnp.real(spectrum).astype(vec_real.dtype)
    spec_imag = jnp.imag(spectrum).astype(vec_real.dtype)
    ratio_real = (spec_real * denom_real + spec_imag * denom_imag) / magnitude
    ratio_imag = (spec_imag * denom_real - spec_real * denom_imag) / magnitude
    result = jnp.fft.ifftn(ratio_real + 1j * ratio_imag)
    return (jnp.real(result).astype(vec_real.dtype), jnp.imag(result).astype(vec_real.dtype))

def inner_product(left_real, left_imag, right_real, right_imag):
    return (jnp.sum(left_real * right_real + left_imag * right_imag), jnp.sum(left_real * right_imag - left_imag * right_real))

def remove_part(vec_real, vec_imag, factor, basis_real, basis_imag):
    return (vec_real - (factor[0] * basis_real - factor[1] * basis_imag), vec_imag - (factor[0] * basis_imag + factor[1] * basis_real))

def small_solve(rhs_norm, first_diag, first_sub, second_top, second_diag, second_sub):
    gram_first = first_diag[0] * first_diag[0] + first_diag[1] * first_diag[1] + first_sub * first_sub
    gram_second = second_top[0] * second_top[0] + second_top[1] * second_top[1] + second_diag[0] * second_diag[0] + second_diag[1] * second_diag[1] + second_sub * second_sub
    cross_real = first_diag[0] * second_top[0] + first_diag[1] * second_top[1] + first_sub * second_diag[0]
    cross_imag = first_diag[0] * second_top[1] - first_diag[1] * second_top[0] + first_sub * second_diag[1]
    target_one = (rhs_norm * first_diag[0], -rhs_norm * first_diag[1])
    target_two = (rhs_norm * second_top[0], -rhs_norm * second_top[1])
    determinant = gram_first * gram_second - (cross_real * cross_real + cross_imag * cross_imag)
    coef_one = ((gram_second * target_one[0] - (cross_real * target_two[0] - cross_imag * target_two[1])) / determinant, (gram_second * target_one[1] - (cross_real * target_two[1] + cross_imag * target_two[0])) / determinant)
    coef_two = ((gram_first * target_two[0] - (cross_real * target_one[0] + cross_imag * target_one[1])) / determinant, (gram_first * target_two[1] - (cross_real * target_one[1] - cross_imag * target_one[0])) / determinant)
    return (coef_one, coef_two)

def krylov_solve(rhs_real, rhs_imag, terms, shift, mean_kappa):
    rhs_norm = jnp.sqrt(jnp.sum(rhs_real * rhs_real + rhs_imag * rhs_imag))
    first_real, first_imag = (rhs_real / rhs_norm, rhs_imag / rhs_norm)
    pre_one = precondition(first_real, first_imag, shift, mean_kappa)
    work_real, work_imag = apply_system(pre_one[0], pre_one[1], terms, shift)
    first_diag = inner_product(first_real, first_imag, work_real, work_imag)
    work_real, work_imag = remove_part(work_real, work_imag, first_diag, first_real, first_imag)
    first_sub = jnp.sqrt(jnp.sum(work_real * work_real + work_imag * work_imag))
    second_real, second_imag = (work_real / first_sub, work_imag / first_sub)
    pre_two = precondition(second_real, second_imag, shift, mean_kappa)
    work_real, work_imag = apply_system(pre_two[0], pre_two[1], terms, shift)
    second_top = inner_product(first_real, first_imag, work_real, work_imag)
    work_real, work_imag = remove_part(work_real, work_imag, second_top, first_real, first_imag)
    second_diag = inner_product(second_real, second_imag, work_real, work_imag)
    work_real, work_imag = remove_part(work_real, work_imag, second_diag, second_real, second_imag)
    second_sub = jnp.sqrt(jnp.sum(work_real * work_real + work_imag * work_imag))
    coef_one, coef_two = small_solve(rhs_norm, first_diag, first_sub, second_top, second_diag, second_sub)
    sol_real = coef_one[0] * pre_one[0] - coef_one[1] * pre_one[1] + coef_two[0] * pre_two[0] - coef_two[1] * pre_two[1]
    sol_imag = coef_one[0] * pre_one[1] + coef_one[1] * pre_one[0] + coef_two[0] * pre_two[1] + coef_two[1] * pre_two[0]
    return (sol_real, sol_imag)

def reference(source, initial, diffusivity):
    steps = source.shape[0]
    terms = face_terms(diffusivity)
    mean_kappa = jnp.mean(diffusivity)
    lifted = step_length * source
    lifted = lifted.at[0].add(initial)
    ramp = jnp.arange(steps, dtype=source.dtype) / steps
    lifted = lifted * (alpha_corner ** ramp)[:, None, None, None]
    spectrum = jnp.fft.fft(lifted, axis=0)
    decay_root = alpha_corner ** (1.0 / steps)
    solved = []
    for frequency in range(steps):
        phase_angle = 2.0 * math.pi * frequency / steps
        shift = (1.0 - decay_root * math.cos(phase_angle), decay_root * math.sin(phase_angle))
        rhs_real = jnp.real(spectrum[frequency]).astype(source.dtype)
        rhs_imag = jnp.imag(spectrum[frequency]).astype(source.dtype)
        sol_real, sol_imag = krylov_solve(rhs_real, rhs_imag, terms, shift, mean_kappa)
        solved.append(sol_real + 1j * sol_imag)
    restored = jnp.fft.ifft(jnp.stack(solved), axis=0)
    return jnp.real(restored).astype(source.dtype) * (alpha_corner ** (-ramp))[:, None, None, None]
```

```python
import functools
import math

import jax
import jax.numpy as jnp
import ml_dtypes
import numpy as np
from jax import lax
from jax.experimental import pallas as pl
from jax.experimental.pallas import tpu as pltpu
from jax.sharding import Mesh, PartitionSpec as P

alpha_corner = 0.05
step_length = 1.0
vmem_bytes = 56 * 1024 * 1024


def real_basis(length):
    place = np.arange(length)
    angle = 2.0 * np.pi * ((place[:, None] * place[None, :]) % length) / length
    basis = np.where(place[None, :] <= length // 2, np.cos(angle), np.sin(angle))
    return basis / np.sqrt(np.sum(basis * basis, axis=0, keepdims=True))


def wave_symbol(length):
    return 4.0 * np.sin(np.pi * np.arange(length) / length) ** 2


def split_table(table, axis, order):
    high = table.astype(ml_dtypes.bfloat16)
    low = (table - high.astype(np.float64)).astype(ml_dtypes.bfloat16)
    return np.concatenate([high if part == "h" else low for part in order], axis=axis)


def sine_basis(count):
    place = np.arange(1, count + 1)
    return np.sqrt(2.0 / (count + 1)) * np.sin(np.pi * np.outer(place, place) / (count + 1))


def sine_symbol(count):
    return 4.0 * np.sin(np.pi * np.arange(1, count + 1) / (2 * (count + 1))) ** 2


def weighted(factors, values):
    total = None
    for factor, value in zip(factors, values):
        term = float(factor) * value
        total = term if total is None else total + term
    return total


def sine_apply(basis, values):
    count = len(values)
    half = count // 2
    even = [values[j] + values[count - 1 - j] for j in range(half)]
    odd = [values[j] - values[count - 1 - j] for j in range(half)]
    if count % 2:
        even.append(values[half])
    return [
        weighted(basis[k, : len(even)], even) if k % 2 == 0 else weighted(basis[k, :half], odd)
        for k in range(count)
    ]


def halves(values):
    high = values.astype(jnp.bfloat16)
    return high, (values - high.astype(jnp.float32)).astype(jnp.bfloat16)


def left_multiply(table, values):
    high, low = halves(values)
    return jnp.dot(
        table, jnp.concatenate([high, high, low], axis=0), preferred_element_type=jnp.float32
    )


def right_multiply(values, table):
    high, low = halves(values)
    return jnp.dot(
        jnp.concatenate([high, low, high], axis=1), table, preferred_element_type=jnp.float32
    )


def inverse_factors(scalars, symbol):
    shift_a, shift_b, shift_i, mean = scalars[0], scalars[1], scalars[2], scalars[3]
    diag_a = shift_a + mean * symbol
    diag_b = shift_b + mean * symbol
    scale_a = 1.0 / (diag_a * diag_a + shift_i * shift_i)
    scale_b = 1.0 / (diag_b * diag_b + shift_i * shift_i)
    return diag_a * scale_a, diag_b * scale_b, shift_i * scale_a


def scaled(factors, first, second):
    return (factors[0] * first + factors[2] * second, factors[1] * second - factors[2] * first)


def forward_kernel(sc, vec, table_y, table_z, lam, inner, edge, sent, work):
    _, planes, full_y, full_z = vec.shape
    count = planes - 1
    chunks = sent.shape[0]
    rows = full_y // chunks
    basis, symbol = sine_basis(count), sine_symbol(count)

    def plane(index, carry):
        both = jnp.concatenate([vec[0, index], vec[1, index]], axis=1)
        both = left_multiply(table_y[...], both)
        both = jnp.concatenate([both[:, :full_z], both[:, full_z:]], axis=0)
        both = right_multiply(both, table_z[...])
        work[0, index] = both[:full_y]
        work[1, index] = both[full_y:]
        return carry

    lax.fori_loop(0, planes, plane, 0)
    mean = sc[3]

    def chunk(index, carry):
        place = pl.ds(pl.multiple_of(index * rows, rows), rows)
        spec = [sine_apply(basis, [work[c, j, place] for j in range(count)]) for c in range(2)]
        first, last = [None, None], [None, None]
        for k in range(count):
            factors = inverse_factors(sc, lam[place] + float(symbol[k]))
            for c, value in enumerate(scaled(factors, spec[0][k], spec[1][k])):
                inner[c, k, place] = value
                low = float(basis[0, k]) * value
                high = float(basis[count - 1, k]) * value
                first[c] = low if k == 0 else first[c] + low
                last[c] = high if k == 0 else last[c] + high
        for c in range(2):
            own = work[c, count, place]
            edge[c, place] = own
            sent[index, c] = own + mean * last[c]
            sent[index, 2 + c] = mean * first[c]
        return carry

    lax.fori_loop(0, chunks, chunk, 0)


def reduced_kernel(sc, waves, table, lam, got, back, spec):
    nodes = got.shape[0]
    per_node = waves.shape[1]
    lam_value = lam[...]

    def forward(mode, carry):
        values = []
        for c in range(2):
            total = None
            for d in range(nodes):
                term = table[d, mode] * (got[d, c] + got[(d + 1) % nodes, 2 + c])
                total = term if total is None else total + term
            values.append(total)
        factors = None
        for part in range(per_node):
            term = inverse_factors(sc, lam_value + waves[mode, part])
            factors = term if factors is None else [a + b for a, b in zip(factors, term)]
        first, second = scaled(factors, values[0], values[1])
        spec[mode, 0] = first * (1.0 / per_node)
        spec[mode, 1] = second * (1.0 / per_node)
        return carry

    lax.fori_loop(0, nodes, forward, 0)

    def backward(node, carry):
        after = lax.rem(node + 1, nodes)
        for c in range(2):
            total = None
            for mode in range(nodes):
                term = table[node, mode] * spec[mode, c]
                total = term if total is None else total + term
            back[node, c] = total
            back[after, 2 + c] = total
        return carry

    lax.fori_loop(0, nodes, backward, 0)


def turn(values, amount, axis):
    return pltpu.roll(values, amount % values.shape[axis], axis)


def folded(values):
    return jnp.sum(values.reshape(-1, 8, values.shape[-1]), axis=0)


def backward_kernel(second, sc, inner, edge, got, lam, table_y, table_z, kappa, rhs, *rest):
    if second:
        prior, prior_out, pre, dots, work = rest
    else:
        pre, out, dots, work = rest
    _, count, full_y, full_z = inner.shape
    planes = count + 1
    chunks = got.shape[0]
    rows = full_y // chunks
    basis, symbol = sine_basis(count), sine_symbol(count)
    shift_a, shift_b, shift_i, mean = sc[0], sc[1], sc[2], sc[3]

    def chunk(index, carry):
        place = pl.ds(pl.multiple_of(index * rows, rows), rows)
        own = [got[index, c] for c in range(2)]
        before = [got[index, 2 + c] for c in range(2)]
        lam_value = lam[place]
        spec = [[], []]
        for k in range(count):
            factors = inverse_factors(sc, lam_value + float(symbol[k]))
            ends = [
                mean * (float(basis[0, k]) * before[c] + float(basis[count - 1, k]) * own[c])
                for c in range(2)
            ]
            for c, value in enumerate(scaled(factors, ends[0], ends[1])):
                spec[c].append(inner[c, k, place] + value)
        diag = mean * (lam_value + 2.0)
        lifted = (
            (shift_a + diag) * own[0] - shift_i * own[1],
            (shift_b + diag) * own[1] + shift_i * own[0],
        )
        for c in range(2):
            values = sine_apply(basis, spec[c])
            for j in range(count):
                work[c, 1 + j, place] = values[j]
            work[c, 0, place] = before[c]
            work[c, planes, place] = own[c]
            work[c, planes + 1, place] = (lifted[c] - edge[c, place]) / mean - values[count - 1]
        return carry

    lax.fori_loop(0, chunks, chunk, 0)

    def plane(index, carry):
        both = jnp.concatenate([work[0, index], work[1, index]], axis=0)
        both = right_multiply(both, table_z[...])
        both = jnp.concatenate([both[:full_y], both[full_y:]], axis=1)
        both = left_multiply(table_y[...], both)
        value = [both[:, :full_z], both[:, full_z:]]
        if second:
            old = [prior[0, index], prior[1, index]]
            value = [
                value[0] - (sc[4] * old[0] - sc[6] * old[1]),
                value[1] - (sc[5] * old[1] + sc[6] * old[0]),
            ]
        pre[0, index] = value[0]
        pre[1, index] = value[1]
        return carry

    lax.fori_loop(0, planes + 2, plane, 0)
    dots[...] = jnp.zeros_like(dots)

    def stencil(index, carry):
        mid = kappa[index + 1]
        face_after = 0.5 * (mid + kappa[index + 2])
        face_before = 0.5 * (mid + kappa[index])
        face_y = 0.5 * (mid + turn(mid, -1, 0))
        face_z = 0.5 * (mid + turn(mid, -1, 1))
        here = [pre[c, index + 1] for c in range(2)]
        result = []
        for c in range(2):
            total = face_after * (here[c] - pre[c, index + 2])
            total = total + face_before * (here[c] - pre[c, index])
            flux = face_y * (here[c] - turn(here[c], -1, 0))
            total = total + (flux - turn(flux, 1, 0))
            flux = face_z * (here[c] - turn(here[c], -1, 1))
            total = total + (flux - turn(flux, 1, 1))
            result.append(step_length * total)
        result[0] = result[0] + (shift_a * here[0] - shift_i * here[1])
        result[1] = result[1] + (shift_b * here[1] + shift_i * here[0])
        base = [rhs[0, index], rhs[1, index]]
        pairs = [(base[0], result[0]), (base[1], result[1])]
        pairs += [(base[0], result[1]), (base[1], result[0])]
        pairs += [(result[0], result[0]), (result[1], result[1])]
        if second:
            old = [prior_out[0, index], prior_out[1, index]]
            rest_a = old[0] - (sc[4] * base[0] - sc[6] * base[1])
            rest_b = old[1] - (sc[5] * base[1] + sc[6] * base[0])
            pairs += [(rest_a, result[0]), (rest_b, result[1])]
            pairs += [(rest_a, result[1]), (rest_b, result[0])]
            pairs += [(rest_a, rest_a), (rest_b, rest_b)]
        else:
            out[0, index] = result[0]
            out[1, index] = result[1]
            pairs += [(base[0], base[0]), (base[1], base[1])]
        for number, (left, right) in enumerate(pairs):
            dots[number] += folded(left * right)
        return carry

    lax.fori_loop(0, planes, stencil, 0)


smem = pl.BlockSpec(memory_space=pltpu.SMEM)
vmem = pl.BlockSpec(memory_space=pltpu.VMEM)
params = pltpu.CompilerParams(vmem_limit_bytes=vmem_bytes)


def wide(*shape):
    return jax.ShapeDtypeStruct(shape, jnp.float32)


class Tables:
    def __init__(self, full_x, full_y, full_z, nodes):
        basis_y, basis_z = real_basis(full_y), real_basis(full_z)
        self.y_forward = split_table(basis_y.T, 1, "hlh")
        self.y_back = split_table(basis_y, 1, "hlh")
        self.z_forward = split_table(basis_z, 0, "hhl")
        self.z_back = split_table(basis_z.T, 0, "hhl")
        lam = wave_symbol(full_y)[:, None] + wave_symbol(full_z)[None, :]
        self.lam = lam.astype(np.float32)
        self.nodes = nodes
        waves = wave_symbol(full_x).reshape(full_x // nodes, nodes).T
        self.waves = np.ascontiguousarray(waves).astype(np.float32)
        self.over_nodes = real_basis(nodes).astype(np.float32)


def precondition(scalars, vec, tables, position):
    _, planes, full_y, full_z = vec.shape
    nodes = tables.nodes
    rows = full_y // nodes
    inner, edge, sent = pl.pallas_call(
        forward_kernel,
        out_shape=(
            wide(2, planes - 1, full_y, full_z),
            wide(2, full_y, full_z),
            wide(nodes, 4, rows, full_z),
        ),
        in_specs=[smem] + [vmem] * 4,
        out_specs=(vmem, vmem, vmem),
        scratch_shapes=[pltpu.VMEM(vec.shape, jnp.float32)],
        compiler_params=params,
        name="forward",
    )(scalars, vec, tables.y_forward, tables.z_forward, tables.lam)
    got = lax.all_to_all(sent, ("space", "x"), split_axis=0, concat_axis=0, tiled=True)
    lam_rows = lax.dynamic_slice_in_dim(jnp.asarray(tables.lam), position * rows, rows, 0)
    back = pl.pallas_call(
        reduced_kernel,
        out_shape=wide(nodes, 4, rows, full_z),
        in_specs=[smem] * 3 + [vmem] * 2,
        out_specs=vmem,
        scratch_shapes=[pltpu.VMEM((nodes, 2, rows, full_z), jnp.float32)],
        compiler_params=params,
        name="reduced",
    )(scalars, tables.waves, tables.over_nodes, lam_rows, got)
    got = lax.all_to_all(back, ("space", "x"), split_axis=0, concat_axis=0, tiled=True)
    return inner, edge, got


def apply_back(second, scalars, parts, tables, kappa, rhs, prior=()):
    _, planes, full_y, full_z = rhs.shape
    halo = wide(2, planes + 2, full_y, full_z)
    dots = wide(12 if second else 8, 8, full_z)
    out_shape = (halo, dots) if second else (halo, wide(*rhs.shape), dots)
    return pl.pallas_call(
        functools.partial(backward_kernel, second),
        out_shape=out_shape,
        in_specs=[smem] + [vmem] * (8 + len(prior)),
        out_specs=(vmem,) * len(out_shape),
        scratch_shapes=[pltpu.VMEM(halo.shape, jnp.float32)],
        compiler_params=params,
        name="backward_second" if second else "backward_first",
    )(
        scalars, *parts, tables.lam, tables.y_back, tables.z_back, kappa, rhs, *prior
    )


def reduced_sums(dots):
    return lax.psum(jnp.sum(dots, axis=(1, 2)), ("space", "x"))


def hermitian(mixed, d00, d11, d01, d10):
    return d00 + mixed * d11, d11 + mixed * d00, mixed * (d01 - d10)


def small_solve(norm2, h11, h21_2, h12, h22, gram_second):
    gram_first = h11[0] * h11[0] + h11[1] * h11[1] + h21_2
    sub = jnp.sqrt(h21_2)
    cross_real = h11[0] * h12[0] + h11[1] * h12[1] + sub * h22[0]
    cross_imag = h11[0] * h12[1] - h11[1] * h12[0] + sub * h22[1]
    norm = jnp.sqrt(norm2)
    one = (norm * h11[0], -norm * h11[1])
    two = (norm * h12[0], -norm * h12[1])
    det = gram_first * gram_second - (cross_real * cross_real + cross_imag * cross_imag)
    c1 = (
        (gram_second * one[0] - (cross_real * two[0] - cross_imag * two[1])) / det,
        (gram_second * one[1] - (cross_real * two[1] + cross_imag * two[0])) / det,
    )
    c2 = (
        (gram_first * two[0] - (cross_real * one[0] + cross_imag * one[1])) / det,
        (gram_first * two[1] - (cross_real * one[1] - cross_imag * one[0])) / det,
    )
    return c1, c2


def solve_pair(rhs, kappa, shifts, mixed, mean, tables, position):
    zero = jnp.zeros((), jnp.float32)
    scalars = jnp.stack([*shifts, mean, zero, zero, zero, zero])
    parts = precondition(scalars, rhs, tables, position)
    pre_one, out_one, dots = apply_back(False, scalars, parts, tables, kappa, rhs)
    sums = reduced_sums(dots)
    norm_a, norm_b, _ = hermitian(mixed, sums[6], sums[7], zero, zero)
    top = hermitian(mixed, sums[0], sums[1], sums[2], sums[3])
    h_a, h_b, h_i = top[0] / norm_a, top[1] / norm_b, top[2] / norm_a
    parts = precondition(scalars, out_one, tables, position)
    scalars = jnp.stack([*shifts, mean, h_a, h_b, h_i, zero])
    pre_two, dots = apply_back(
        True, scalars, parts, tables, kappa, rhs, (pre_one, out_one)
    )
    sums = reduced_sums(dots)
    top = hermitian(mixed, sums[0], sums[1], sums[2], sums[3])
    length = hermitian(mixed, sums[4], sums[5], zero, zero)
    diag = hermitian(mixed, sums[6], sums[7], sums[8], sums[9])
    rest = hermitian(mixed, sums[10], sums[11], zero, zero)
    coefs = []
    for which, norm2, h_r in ((0, norm_a, h_a), (1, norm_b, h_b)):
        rest2 = rest[which]
        c1, c2 = small_solve(
            norm2,
            (h_r, h_i),
            rest2 / norm2,
            [part / jnp.sqrt(norm2 * rest2) for part in (top[which], top[2])],
            [part / rest2 for part in (diag[which], diag[2])],
            length[which] / rest2,
        )
        scale_one, scale_two = 1.0 / jnp.sqrt(norm2), 1.0 / jnp.sqrt(rest2)
        coefs.append((c1[0] * scale_one, c1[1] * scale_one, c2[0] * scale_two, c2[1] * scale_two))
    one, two = pre_one[:, 1:-1], pre_two[:, 1:-1]
    ca, cb = coefs
    return jnp.stack(
        [
            ca[0] * one[0] - ca[1] * one[1] + ca[2] * two[0] - ca[3] * two[1],
            cb[0] * one[1] + cb[1] * one[0] + cb[2] * two[1] + cb[3] * two[0],
        ]
    )


def shards(cores, source, initial, diffusivity):
    chips = lax.axis_size("x")
    steps = chips * cores
    space = lax.axis_size("space")
    nodes = space * chips
    chip, core = lax.axis_index("x"), lax.axis_index("core")
    place = lax.axis_index("space")
    position = place * chips + chip
    step = chip * cores + core
    slab, full_y, full_z = diffusivity.shape
    planes = slab // chips
    full_x = slab * space
    tables = Tables(full_x, full_y, full_z, nodes)

    forward = [(i, (i + 1) % space) for i in range(space)]
    backward = [(b, a) for a, b in forward]
    low = lax.ppermute(diffusivity[-1:], "space", forward)
    high = lax.ppermute(diffusivity[:1], "space", backward)
    padded = jnp.concatenate([low, diffusivity, high], axis=0)
    kappa = lax.dynamic_slice_in_dim(padded, chip * planes, planes + 2, 0)
    mean = lax.psum(jnp.sum(diffusivity), "space") / (full_x * full_y * full_z)

    lifted = step_length * source[0] + jnp.where(step == 0, 1.0, 0.0) * initial
    lifted = lifted * jnp.power(alpha_corner, step.astype(jnp.float32) / steps)
    mine = lax.all_to_all(lifted, "x", split_axis=0, concat_axis=0, tiled=True)
    mine = mine.reshape(chips, planes, full_y, full_z)
    swap = [(i, cores - 1 - i) for i in range(cores)]
    other = lax.ppermute(mine, "core", swap)

    pairs = steps // 2
    per_core = pairs // cores
    angle = 2.0 * np.pi * np.outer(np.arange(steps), np.arange(pairs)) / steps
    to_pairs = np.stack([np.cos(angle), -np.sin(angle)], axis=2)
    to_pairs[:, 0, 1] = (-1.0) ** np.arange(steps)
    from_pairs = 2.0 * to_pairs / steps
    from_pairs[:, 0] = to_pairs[:, 0] / steps
    to_pairs = jnp.asarray(to_pairs.astype(np.float32).reshape(chips, cores, cores, per_core, 2))
    from_pairs = jnp.asarray(
        from_pairs.astype(np.float32).reshape(chips, cores, cores, per_core, 2)
    )
    to_mine = lax.dynamic_index_in_dim(to_pairs, core, 2, False)
    to_mine_own = lax.dynamic_index_in_dim(to_mine, core, 1, False)
    to_mine_other = lax.dynamic_index_in_dim(to_mine, cores - 1 - core, 1, False)
    solved = []
    decay_root = alpha_corner ** (1.0 / steps)
    for pair in range(per_core):
        rhs = jnp.stack(
            [
                sum(
                    to_mine_own[n, pair, c] * mine[n] + to_mine_other[n, pair, c] * other[n]
                    for n in range(chips)
                )
                for c in range(2)
            ]
        )
        number = core * per_core + pair
        turn_angle = 2.0 * math.pi * number.astype(jnp.float32) / steps
        mixed = jnp.where(number == 0, 0.0, 1.0)
        shift_a = 1.0 - decay_root * jnp.cos(turn_angle)
        shift_b = jnp.where(number == 0, 1.0 + decay_root, shift_a)
        shift_i = mixed * decay_root * jnp.sin(turn_angle)
        solved.append(
            solve_pair(rhs, kappa, (shift_a, shift_b, shift_i), mixed, mean, tables, position)
        )
    solved = jnp.stack(solved)
    other = lax.ppermute(solved, "core", swap)
    from_core = lax.dynamic_index_in_dim(from_pairs, core, 1, False)
    from_own = lax.dynamic_index_in_dim(from_core, core, 1, False)
    from_other = lax.dynamic_index_in_dim(from_core, cores - 1 - core, 1, False)
    decay = jnp.power(
        alpha_corner, -(jnp.arange(chips) * cores + core).astype(jnp.float32) / steps
    )
    fields = jnp.concatenate(
        [
            decay[n]
            * sum(
                from_own[n, pair, c] * solved[pair, c] + from_other[n, pair, c] * other[pair, c]
                for pair in range(per_core)
                for c in range(2)
            )
            for n in range(chips)
        ]
    )
    field_out = lax.all_to_all(fields, "x", split_axis=0, concat_axis=0, tiled=True)
    return field_out[None]


def solution(mesh):
    cores = 2
    steps = mesh.shape["tm"]
    split = Mesh(
        mesh.devices.reshape(steps // cores, cores, mesh.shape["space"]), ("x", "core", "space")
    )
    in_specs = (P(("x", "core"), "space"), P("space"), P("space"))
    out_specs = P(("x", "core"), "space")
    return jax.shard_map(
        functools.partial(shards, cores),
        mesh=split,
        in_specs=in_specs,
        out_specs=out_specs,
        check_vma=False,
    )
```

```python
import functools
import math

import jax
import jax.numpy as jnp
import ml_dtypes
import numpy as np
from jax import lax
from jax.experimental import pallas as pl
from jax.experimental.pallas import tpu as pltpu
from jax.sharding import Mesh, PartitionSpec as P

alpha_corner = 0.05
step_length = 1.0
vmem_bytes = 56 * 1024 * 1024


def real_basis(length):
    place = np.arange(length)
    angle = 2.0 * np.pi * ((place[:, None] * place[None, :]) % length) / length
    basis = np.where(place[None, :] <= length // 2, np.cos(angle), np.sin(angle))
    return basis / np.sqrt(np.sum(basis * basis, axis=0, keepdims=True))


def wave_symbol(length):
    return 4.0 * np.sin(np.pi * np.arange(length) / length) ** 2


def split_table(table, axis, order):
    high = table.astype(ml_dtypes.bfloat16)
    low = (table - high.astype(np.float64)).astype(ml_dtypes.bfloat16)
    return np.concatenate([high if part == "h" else low for part in order], axis=axis)


def sine_basis(count):
    place = np.arange(1, count + 1)
    return np.sqrt(2.0 / (count + 1)) * np.sin(np.pi * np.outer(place, place) / (count + 1))


def sine_symbol(count):
    return 4.0 * np.sin(np.pi * np.arange(1, count + 1) / (2 * (count + 1))) ** 2


def weighted(factors, values):
    total = None
    for factor, value in zip(factors, values):
        term = float(factor) * value
        total = term if total is None else total + term
    return total


def sine_apply(basis, values):
    count = len(values)
    half = count // 2
    even = [values[j] + values[count - 1 - j] for j in range(half)]
    odd = [values[j] - values[count - 1 - j] for j in range(half)]
    if count % 2:
        even.append(values[half])
    return [
        weighted(basis[k, : len(even)], even) if k % 2 == 0 else weighted(basis[k, :half], odd)
        for k in range(count)
    ]


def halves(values):
    high = values.astype(jnp.bfloat16)
    return high, (values - high.astype(jnp.float32)).astype(jnp.bfloat16)


def left_multiply(table, values):
    high, low = halves(values)
    return jnp.dot(
        table, jnp.concatenate([high, high, low], axis=0), preferred_element_type=jnp.float32
    )


def right_multiply(values, table):
    high, low = halves(values)
    return jnp.dot(
        jnp.concatenate([high, low, high], axis=1), table, preferred_element_type=jnp.float32
    )


def inverse_factors(scalars, symbol):
    shift_a, shift_b, shift_i, mean = scalars[:4]
    diag_a = shift_a + mean * symbol
    diag_b = shift_b + mean * symbol
    scale_a = 1.0 / (diag_a * diag_a + shift_i * shift_i)
    scale_b = 1.0 / (diag_b * diag_b + shift_i * shift_i)
    return diag_a * scale_a, diag_b * scale_b, shift_i * scale_a


def scaled(factors, first, second):
    return (factors[0] * first + factors[2] * second, factors[1] * second - factors[2] * first)


def row(ref, number):
    return ref[pl.ds(number, 1), :]


def transform_plane(first, second, table_y, table_z, work, index):
    full_y, full_z = first.shape
    both = jnp.concatenate([first, second], axis=1)
    both = left_multiply(table_y[...], both)
    both = jnp.concatenate([both[:, :full_z], both[:, full_z:]], axis=0)
    both = right_multiply(both, table_z[...])
    work[0, index] = both[:full_y]
    work[1, index] = both[full_y:]


def inner_solve(sc, lam, work, inner, edge, sent):
    _, planes, full_y, _ = work.shape
    count = planes - 1
    chunks = sent.shape[0]
    rows = full_y // chunks
    basis, symbol = sine_basis(count), sine_symbol(count)
    scalars = [row(sc, number) for number in range(4)]
    mean = scalars[3]

    def chunk(index, carry):
        place = pl.ds(pl.multiple_of(index * rows, rows), rows)
        spec = [sine_apply(basis, [work[c, j, place] for j in range(count)]) for c in range(2)]
        first, last = [None, None], [None, None]
        for k in range(count):
            factors = inverse_factors(scalars, lam[place] + float(symbol[k]))
            for c, value in enumerate(scaled(factors, spec[0][k], spec[1][k])):
                inner[c, k, place] = value
                low = float(basis[0, k]) * value
                high = float(basis[count - 1, k]) * value
                first[c] = low if k == 0 else first[c] + low
                last[c] = high if k == 0 else last[c] + high
        for c in range(2):
            own = work[c, count, place]
            edge[c, place] = own
            sent[index, c] = own + mean * last[c]
            sent[index, 2 + c] = mean * first[c]
        return carry

    lax.fori_loop(0, chunks, chunk, 0)


def loop(start, stop, body):
    def step(index, carry):
        body(index)
        return carry

    lax.fori_loop(start, stop, step, 0)


def remote(src, dst, send, recv, **where):
    return pltpu.make_async_remote_copy(
        src_ref=src,
        dst_ref=dst,
        send_sem=send,
        recv_sem=recv,
        device_id=where,
        device_id_type=pl.DeviceIdType.MESH,
    )


def greet(barrier, **where):
    pl.semaphore_signal(
        barrier, inc=1, device_id=where, device_id_type=pl.DeviceIdType.MESH
    )


def start_kernel(
    geometry, coef, coef_first, base, source, initial, dif, table_y, table_z, lam, *rest
):
    chips, space, per_core = geometry
    outs, scratch = rest[: 1 + 5 * per_core], rest[1 + 5 * per_core :]
    kappa = outs[0]
    groups = [outs[1 + 5 * i : 6 + 5 * i] for i in range(per_core)]
    mine, other, work, low, high, tile, tiles = scratch[:7]
    send_x, recv_x, send_c, recv_c, send_h, recv_h, send_t, recv_t = scratch[7:]
    planes = mine.shape[1]
    cores = 2
    chip, core, place = lax.axis_index("x"), lax.axis_index("core"), lax.axis_index("space")
    twin = cores - 1 - core

    barrier = pltpu.get_barrier_semaphore()
    for j in range(1, chips):
        greet(barrier, x=lax.rem(chip + j, chips))
    for j in range(1, space):
        greet(barrier, space=lax.rem(place + j, space))
    greet(barrier, core=twin)
    pl.semaphore_wait(barrier, chips + space - 1)

    def to_chip(j, index):
        peer = lax.rem(chip + j, chips)
        return remote(
            source.at[0, peer * planes + index],
            mine.at[chip, index],
            send_x.at[j, index],
            recv_x.at[j, index],
            x=peer,
        )

    def own_to_core(index):
        return remote(
            source.at[0, chip * planes + index],
            other.at[chip, index],
            send_c.at[0, index],
            recv_c.at[0, index],
            core=twin,
        )

    def to_core(j, index):
        sender = lax.rem(chip + chips - j, chips)
        return remote(
            mine.at[sender, index],
            other.at[sender, index],
            send_c.at[j, index],
            recv_c.at[j, index],
            core=twin,
        )

    def begin(index):
        for j in range(1, chips):
            to_chip(j, index).start()

    loop(0, planes, begin)
    loop(0, planes, lambda index: own_to_core(index).start())
    slab = dif.shape[0]
    after, before = lax.rem(place + 1, space), lax.rem(place + space - 1, space)
    up = remote(dif.at[slab - 1], low, send_h.at[0], recv_h.at[0], space=after)
    down = remote(dif.at[0], high, send_h.at[1], recv_h.at[1], space=before)
    up.start()
    down.start()
    tile[...] = jnp.zeros_like(tile)

    def add_plane(index):
        tile[...] += folded(dif[index])
        return None

    loop(0, slab, add_plane)
    shares = [
        remote(
            tile,
            tiles.at[place],
            send_t.at[j],
            recv_t.at[j],
            space=lax.rem(place + j, space),
        )
        for j in range(1, space)
    ]
    for share in shares:
        share.start()
    tiles[place] = tile[...]

    def keep(index):
        mine[chip, index] = source[0, chip * planes + index]

    loop(0, planes, keep)

    def relay(index):
        for j in range(1, chips):
            to_chip(j, index).wait_recv()
            to_core(j, index).start()

    def process(index):
        own_to_core(index).wait_recv()
        for j in range(1, chips):
            to_core(j, index).wait_recv()
        opening = initial[chip * planes + index]
        for i in range(per_core):
            rhs = groups[i][1]
            values = []
            for c in range(2):
                column = (core * per_core + i) * 2 + c
                total = coef_first[0, column] * opening
                for n in range(chips):
                    total = total + coef[n * cores + core, column] * mine[n, index]
                    total = total + coef[n * cores + twin, column] * other[n, index]
                rhs[c, index] = total
                values.append(total)
            transform_plane(values[0], values[1], table_y, table_z, work.at[i], index)

    relay(0)

    def both(index):
        relay(index + 1)
        process(index)

    loop(0, planes - 1, both)
    process(planes - 1)

    for share in shares:
        share.wait_recv()
    total = tiles[0]
    for j in range(1, space):
        total = total + tiles[j]
    total = jnp.sum(jnp.sum(total, axis=0, keepdims=True), axis=1, keepdims=True)
    cells = slab * space * dif.shape[1] * dif.shape[2]
    for i in range(per_core):
        sc = groups[i][0]
        sc[...] = base[core * per_core + i]
        sc[pl.ds(3, 1), :] = jnp.broadcast_to(total / cells, (1, sc.shape[1]))
    up.wait_recv()
    down.wait_recv()
    first = chip * planes
    kappa[0] = jnp.where(chip > 0, dif[jnp.maximum(first - 1, 0)], low[...])
    kappa[planes + 1] = jnp.where(
        chip < chips - 1, dif[jnp.minimum(first + planes, slab - 1)], high[...]
    )

    def keep_kappa(index):
        kappa[index + 1] = dif[first + index]

    loop(0, planes, keep_kappa)
    for i in range(per_core):
        sc, _, inner, edge, sent = groups[i]
        inner_solve(sc, lam, work.at[i], inner, edge, sent)

    up.wait_send()
    down.wait_send()
    for share in shares:
        share.wait_send()

    def end(index):
        own_to_core(index).wait_send()
        for j in range(1, chips):
            to_chip(j, index).wait_send()
            to_core(j, index).wait_send()

    loop(0, planes, end)


def node_place(node, chips):
    return {"space": lax.div(node, chips), "x": lax.rem(node, chips)}


def share_dots(dots, tile, tiles, send, recv, nodes, chips, position):
    tile[...] = jnp.zeros(tile.shape, jnp.float32)
    for number in range(dots.shape[0]):
        tile[pl.ds(number, 1), :] = jnp.sum(dots[number], axis=0, keepdims=True)

    def one(j):
        peer = lax.rem(position + j, nodes)
        return remote(tile, tiles.at[position], send.at[j], recv.at[j], **node_place(peer, chips))

    loop(1, nodes, lambda j: one(j).start())
    tiles[position] = tile[...]
    return one


def dot_rows(tiles, nodes, count):
    total = tiles[0]
    for node in range(1, nodes):
        total = total + tiles[node]
    total = jnp.sum(total, axis=1, keepdims=True)
    return [
        jnp.broadcast_to(total[number : number + 1], (1, tiles.shape[2]))
        for number in range(count)
    ]


def greet_nodes(nodes, chips, position):
    barrier = pltpu.get_barrier_semaphore()
    loop(
        1,
        nodes,
        lambda j: greet(barrier, **node_place(lax.rem(position + j, nodes), chips)),
    )
    pl.semaphore_wait(barrier, nodes - 1)


def exchange_kernel(chips, second, sc, waves, table, lam, sent, *rest):
    if second:
        dots, res, sc_out, got, back, spec, tile, tiles = rest[:8]
        send, recv, send_b, recv_b, send_t, recv_t = rest[8:]
    else:
        res, got, back, spec, send, recv, send_b, recv_b = rest
    nodes, _, rows, _ = sent.shape
    per_node = waves.shape[1]
    position = lax.axis_index("space") * chips + lax.axis_index("x")
    greet_nodes(nodes, chips, position)

    def out(j):
        peer = lax.rem(position + j, nodes)
        return remote(
            sent.at[peer], got.at[position], send.at[j], recv.at[j], **node_place(peer, chips)
        )

    def home(j):
        peer = lax.rem(position + j, nodes)
        return remote(
            back.at[peer],
            res.at[position],
            send_b.at[j],
            recv_b.at[j],
            **node_place(peer, chips),
        )

    loop(1, nodes, lambda j: out(j).start())
    if second:
        share = share_dots(dots, tile, tiles, send_t, recv_t, nodes, chips, position)
    got[position] = sent[position]
    loop(1, nodes, lambda j: out(j).wait_recv())

    scalars = [row(sc, number) for number in range(4)]
    lam_value = lam[pl.ds(pl.multiple_of(position * rows, rows), rows)]

    def forward(mode):
        values = []
        for c in range(2):
            total = None
            for d in range(nodes):
                term = table[d, mode] * (got[d, c] + got[(d + 1) % nodes, 2 + c])
                total = term if total is None else total + term
            values.append(total)
        factors = None
        for part in range(per_node):
            term = inverse_factors(scalars, lam_value + waves[mode, part])
            factors = term if factors is None else [a + b for a, b in zip(factors, term)]
        first, second_value = scaled(factors, values[0], values[1])
        spec[mode, 0] = first * (1.0 / per_node)
        spec[mode, 1] = second_value * (1.0 / per_node)

    loop(0, nodes, forward)

    def backward(j):
        node = lax.rem(position + j, nodes)
        after = lax.rem(node + 1, nodes)
        for c in range(2):
            total = None
            for mode in range(nodes):
                term = table[node, mode] * spec[mode, c]
                total = term if total is None else total + term
            back[node, c] = total
            back[after, 2 + c] = total

    backward(0)

    def send_home(j):
        backward(j)
        home(j).start()

    loop(1, nodes, send_home)
    res[position] = back[position]
    if second:
        loop(1, nodes, lambda j: share(j).wait_recv())
        sums = dot_rows(tiles, nodes, 8)
        mixed = row(sc, 4)
        norm_a, norm_b, _ = hermitian(mixed, sums[6], sums[7], sums[6], sums[6])
        top = hermitian(mixed, sums[0], sums[1], sums[2], sums[3])
        sc_out[...] = sc[...]
        values = (top[0] / norm_a, top[1] / norm_b, top[2] / norm_a, norm_a, norm_b)
        for number, value in enumerate(values):
            sc_out[pl.ds(5 + number, 1), :] = value
        loop(1, nodes, lambda j: share(j).wait_send())

    def end(j):
        home(j).wait_recv()
        home(j).wait_send()
        out(j).wait_send()

    loop(1, nodes, end)


def pair_coefs(sc, tiles, nodes):
    sums = dot_rows(tiles, nodes, 12)
    mixed = row(sc, 4)
    h_i = row(sc, 7)
    top = hermitian(mixed, sums[0], sums[1], sums[2], sums[3])
    length = hermitian(mixed, sums[4], sums[5], sums[4], sums[4])
    diag = hermitian(mixed, sums[6], sums[7], sums[8], sums[9])
    left = hermitian(mixed, sums[10], sums[11], sums[10], sums[10])
    coefs = []
    for which in range(2):
        h_r, norm2, left2 = row(sc, 5 + which), row(sc, 8 + which), left[which]
        root = jnp.sqrt(norm2) * jnp.sqrt(left2)
        c1, c2 = small_solve(
            norm2,
            (h_r, h_i),
            left2 / norm2,
            [part / root for part in (top[which], top[2])],
            [part / left2 for part in (diag[which], diag[2])],
            length[which] / left2,
        )
        scale_one, scale_two = 1.0 / jnp.sqrt(norm2), 1.0 / jnp.sqrt(left2)
        coefs.append((c1[0] * scale_one, c1[1] * scale_one, c2[0] * scale_two, c2[1] * scale_two))
    return coefs


def finish_kernel(geometry, coef, *rest):
    chips, space, per_core = geometry
    groups = [rest[4 * i : 4 * i + 4] for i in range(per_core)]
    out = rest[4 * per_core]
    sol, twin_sol, fields, tile, tiles = rest[4 * per_core + 1 : 4 * per_core + 6]
    send_t, recv_t, send_c, recv_c, send_x, recv_x = rest[4 * per_core + 6 :]
    planes = sol.shape[0]
    cores = 2
    nodes = space * chips
    chip, core = lax.axis_index("x"), lax.axis_index("core")
    position = lax.axis_index("space") * chips + chip
    twin = cores - 1 - core

    barrier = pltpu.get_barrier_semaphore()
    loop(
        1,
        nodes,
        lambda j: greet(barrier, **node_place(lax.rem(position + j, nodes), chips)),
    )
    greet(barrier, core=twin)
    pl.semaphore_wait(barrier, nodes)

    shares = [
        share_dots(
            groups[i][3], tile.at[i], tiles.at[i], send_t.at[i], recv_t.at[i], nodes, chips, position
        )
        for i in range(per_core)
    ]
    coefs = []
    for i in range(per_core):
        loop(1, nodes, lambda j: shares[i](j).wait_recv())
        coefs.append(pair_coefs(groups[i][0], tiles.at[i], nodes))

    def to_core(index):
        return remote(
            sol.at[index], twin_sol.at[index], send_c.at[index], recv_c.at[index], core=twin
        )

    def to_chip(j, index):
        peer = lax.rem(chip + j, chips)
        return remote(
            fields.at[peer, index],
            out.at[0, chip * planes + index],
            send_x.at[j, index],
            recv_x.at[j, index],
            x=peer,
        )

    def combine(index):
        for i in range(per_core):
            _, one, two, _ = groups[i]
            ca, cb = coefs[i]
            one = [one[c, index + 1] for c in range(2)]
            two = [two[c, index + 1] for c in range(2)]
            sol[index, 2 * i] = ca[0] * one[0] - ca[1] * one[1] + ca[2] * two[0] - ca[3] * two[1]
            sol[index, 2 * i + 1] = (
                cb[0] * one[1] + cb[1] * one[0] + cb[2] * two[1] + cb[3] * two[0]
            )
        to_core(index).start()

    def spread(index):
        to_core(index).wait_recv()

        def field(peer):
            total = None
            for part in range(2 * per_core):
                term = coef[peer * cores + core, core * per_core * 2 + part] * sol[index, part]
                term = term + (
                    coef[peer * cores + core, twin * per_core * 2 + part] * twin_sol[index, part]
                )
                total = term if total is None else total + term
            return total

        for j in range(1, chips):
            peer = lax.rem(chip + j, chips)
            fields[peer, index] = field(peer)
            to_chip(j, index).start()
        out[0, chip * planes + index] = field(chip)

    combine(0)

    def both(index):
        combine(index + 1)
        spread(index)

    loop(0, planes - 1, both)
    spread(planes - 1)
    for i in range(per_core):
        loop(1, nodes, lambda j: shares[i](j).wait_send())

    def end(index):
        to_core(index).wait_send()
        for j in range(1, chips):
            to_chip(j, index).wait_send()
            to_chip(j, index).wait_recv()

    loop(0, planes, end)


def turn(values, amount, axis):
    return pltpu.roll(values, amount % values.shape[axis], axis)


def folded(values):
    return jnp.sum(values.reshape(-1, 8, values.shape[-1]), axis=0)


def backward_kernel(second, sc, inner, edge, got, lam, table_y, table_z, kappa, rhs, *rest):
    if second:
        prior, prior_out, pre, dots, work = rest
    else:
        forward_y, forward_z, pre, out, dots, inner_out, edge_out, sent, work, work_out = rest
    _, count, full_y, full_z = inner.shape
    planes = count + 1
    chunks = got.shape[0]
    rows = full_y // chunks
    basis, symbol = sine_basis(count), sine_symbol(count)
    scalars = [row(sc, number) for number in range(4)]
    shift_a, shift_b, shift_i, mean = scalars
    if second:
        h_a, h_b, h_i = [row(sc, number) for number in range(5, 8)]

    def chunk(index, carry):
        place = pl.ds(pl.multiple_of(index * rows, rows), rows)
        own = [got[index, c] for c in range(2)]
        before = [got[index, 2 + c] for c in range(2)]
        lam_value = lam[place]
        spec = [[], []]
        for k in range(count):
            factors = inverse_factors(scalars, lam_value + float(symbol[k]))
            ends = [
                mean * (float(basis[0, k]) * before[c] + float(basis[count - 1, k]) * own[c])
                for c in range(2)
            ]
            for c, value in enumerate(scaled(factors, ends[0], ends[1])):
                spec[c].append(inner[c, k, place] + value)
        diag = mean * (lam_value + 2.0)
        lifted = (
            (shift_a + diag) * own[0] - shift_i * own[1],
            (shift_b + diag) * own[1] + shift_i * own[0],
        )
        for c in range(2):
            values = sine_apply(basis, spec[c])
            for j in range(count):
                work[c, 1 + j, place] = values[j]
            work[c, 0, place] = before[c]
            work[c, planes, place] = own[c]
            work[c, planes + 1, place] = (lifted[c] - edge[c, place]) / mean - values[count - 1]
        return carry

    lax.fori_loop(0, chunks, chunk, 0)

    def plane(index, carry):
        both = jnp.concatenate([work[0, index], work[1, index]], axis=0)
        both = right_multiply(both, table_z[...])
        both = jnp.concatenate([both[:full_y], both[full_y:]], axis=1)
        both = left_multiply(table_y[...], both)
        value = [both[:, :full_z], both[:, full_z:]]
        if second:
            old = [prior[0, index], prior[1, index]]
            value = [
                value[0] - (h_a * old[0] - h_i * old[1]),
                value[1] - (h_b * old[1] + h_i * old[0]),
            ]
        pre[0, index] = value[0]
        pre[1, index] = value[1]
        return carry

    lax.fori_loop(0, planes + 2, plane, 0)
    dots[...] = jnp.zeros_like(dots)

    def stencil(index, carry):
        mid = kappa[index + 1]
        face_after = 0.5 * (mid + kappa[index + 2])
        face_before = 0.5 * (mid + kappa[index])
        face_y = 0.5 * (mid + turn(mid, -1, 0))
        face_z = 0.5 * (mid + turn(mid, -1, 1))
        here = [pre[c, index + 1] for c in range(2)]
        result = []
        for c in range(2):
            total = face_after * (here[c] - pre[c, index + 2])
            total = total + face_before * (here[c] - pre[c, index])
            flux = face_y * (here[c] - turn(here[c], -1, 0))
            total = total + (flux - turn(flux, 1, 0))
            flux = face_z * (here[c] - turn(here[c], -1, 1))
            total = total + (flux - turn(flux, 1, 1))
            result.append(step_length * total)
        result[0] = result[0] + (shift_a * here[0] - shift_i * here[1])
        result[1] = result[1] + (shift_b * here[1] + shift_i * here[0])
        base = [rhs[0, index], rhs[1, index]]
        pairs = [(base[0], result[0]), (base[1], result[1])]
        pairs += [(base[0], result[1]), (base[1], result[0])]
        pairs += [(result[0], result[0]), (result[1], result[1])]
        if second:
            old = [prior_out[0, index], prior_out[1, index]]
            rest_a = old[0] - (h_a * base[0] - h_i * base[1])
            rest_b = old[1] - (h_b * base[1] + h_i * base[0])
            pairs += [(rest_a, result[0]), (rest_b, result[1])]
            pairs += [(rest_a, result[1]), (rest_b, result[0])]
            pairs += [(rest_a, rest_a), (rest_b, rest_b)]
        else:
            out[0, index] = result[0]
            out[1, index] = result[1]
            transform_plane(result[0], result[1], forward_y, forward_z, work_out, index)
            pairs += [(base[0], base[0]), (base[1], base[1])]
        for number, (left, right) in enumerate(pairs):
            dots[number] += folded(left * right)
        return carry

    lax.fori_loop(0, planes, stencil, 0)
    if not second:
        inner_solve(sc, lam, work_out, inner_out, edge_out, sent)


def hermitian(mixed, d00, d11, d01, d10):
    return d00 + mixed * d11, d11 + mixed * d00, mixed * (d01 - d10)


def small_solve(norm2, h11, h21_2, h12, h22, gram_second):
    gram_first = h11[0] * h11[0] + h11[1] * h11[1] + h21_2
    sub = jnp.sqrt(h21_2)
    cross_real = h11[0] * h12[0] + h11[1] * h12[1] + sub * h22[0]
    cross_imag = h11[0] * h12[1] - h11[1] * h12[0] + sub * h22[1]
    norm = jnp.sqrt(norm2)
    one = (norm * h11[0], -norm * h11[1])
    two = (norm * h12[0], -norm * h12[1])
    det = gram_first * gram_second - (cross_real * cross_real + cross_imag * cross_imag)
    c1 = (
        (gram_second * one[0] - (cross_real * two[0] - cross_imag * two[1])) / det,
        (gram_second * one[1] - (cross_real * two[1] + cross_imag * two[0])) / det,
    )
    c2 = (
        (gram_first * two[0] - (cross_real * one[0] + cross_imag * one[1])) / det,
        (gram_first * two[1] - (cross_real * one[1] - cross_imag * one[0])) / det,
    )
    return c1, c2


smem = pl.BlockSpec(memory_space=pltpu.SMEM)
vmem = pl.BlockSpec(memory_space=pltpu.VMEM)
dma = pltpu.SemaphoreType.DMA


def wide(*shape):
    return jax.ShapeDtypeStruct(shape, jnp.float32)


def held(*shape):
    return pltpu.VMEM(shape, jnp.float32)


def params(number=None):
    if number is None:
        return pltpu.CompilerParams(vmem_limit_bytes=vmem_bytes)
    return pltpu.CompilerParams(
        vmem_limit_bytes=vmem_bytes, collective_id=number, has_side_effects=True
    )


class Tables:
    def __init__(self, full_x, full_y, full_z, nodes):
        basis_y, basis_z = real_basis(full_y), real_basis(full_z)
        self.y_forward = split_table(basis_y.T, 1, "hlh")
        self.y_back = split_table(basis_y, 1, "hlh")
        self.z_forward = split_table(basis_z, 0, "hhl")
        self.z_back = split_table(basis_z.T, 0, "hhl")
        lam = wave_symbol(full_y)[:, None] + wave_symbol(full_z)[None, :]
        self.lam = lam.astype(np.float32)
        self.nodes = nodes
        waves = wave_symbol(full_x).reshape(full_x // nodes, nodes).T
        self.waves = np.ascontiguousarray(waves).astype(np.float32)
        self.over_nodes = real_basis(nodes).astype(np.float32)


def exchange(second, geometry, sc, sent, tables, dots=()):
    chips = geometry[0]
    nodes, _, rows, full_z = sent.shape
    out_shape = [wide(*sent.shape)]
    scratch = [held(*sent.shape), held(*sent.shape), held(nodes, 2, rows, full_z)]
    semaphores = [dma((nodes,))] * 4
    if second:
        out_shape.append(wide(16, full_z))
        scratch += [held(16, full_z), held(nodes, 16, full_z)]
        semaphores += [dma((nodes,))] * 2
    return pl.pallas_call(
        functools.partial(exchange_kernel, chips, second),
        out_shape=tuple(out_shape),
        in_specs=[vmem, smem, smem, vmem, vmem] + [vmem] * len(dots),
        out_specs=(vmem,) * len(out_shape),
        scratch_shapes=scratch + semaphores,
        compiler_params=params(2 if second else 1),
        name="exchange_second" if second else "exchange_first",
    )(sc, tables.waves, tables.over_nodes, tables.lam, sent, *dots)


def apply_back(second, sc, inner, edge, got, tables, kappa, rhs, prior=()):
    _, planes, full_y, full_z = rhs.shape
    halo = wide(2, planes + 2, full_y, full_z)
    scratch = [held(*halo.shape)]
    if second:
        out_shape = (halo, wide(12, 8, full_z))
    else:
        prior = (tables.y_forward, tables.z_forward)
        out_shape = (halo, wide(*rhs.shape), wide(8, 8, full_z))
        out_shape += (wide(*inner.shape), wide(*edge.shape), wide(*got.shape))
        scratch.append(held(*rhs.shape))
    return pl.pallas_call(
        functools.partial(backward_kernel, second),
        out_shape=out_shape,
        in_specs=[vmem] * (9 + len(prior)),
        out_specs=(vmem,) * len(out_shape),
        scratch_shapes=scratch,
        compiler_params=params(),
        name="backward_second" if second else "backward_first",
    )(sc, inner, edge, got, tables.lam, tables.y_back, tables.z_back, kappa, rhs, *prior)


def shards(cores, source, initial, diffusivity):
    chips = lax.axis_size("x")
    steps = chips * cores
    space = lax.axis_size("space")
    nodes = space * chips
    slab, full_y, full_z = diffusivity.shape
    planes = slab // chips
    full_x = slab * space
    rows = full_y // nodes
    tables = Tables(full_x, full_y, full_z, nodes)

    pairs = steps // 2
    per_core = pairs // cores
    geometry = (chips, space, per_core)
    angle = 2.0 * np.pi * np.outer(np.arange(steps), np.arange(pairs)) / steps
    to_pairs = np.stack([np.cos(angle), -np.sin(angle)], axis=2)
    to_pairs[:, 0, 1] = (-1.0) ** np.arange(steps)
    from_pairs = 2.0 * to_pairs / steps
    from_pairs[:, 0] = to_pairs[:, 0] / steps
    decay = (alpha_corner ** (np.arange(steps) / steps))[:, None]
    to_pairs = to_pairs.reshape(steps, steps)
    coef_first = to_pairs[:1].astype(np.float32)
    to_pairs = (to_pairs * decay * step_length).astype(np.float32)
    from_pairs = (from_pairs.reshape(steps, steps) / decay).astype(np.float32)
    root = alpha_corner ** (1.0 / steps)
    base = np.zeros((pairs, 16, full_z), np.float32)
    for pair in range(pairs):
        turned = 2.0 * math.pi * pair / steps
        base[pair, 0] = 1.0 - root * math.cos(turned)
        base[pair, 1] = 1.0 + root if pair == 0 else base[pair, 0]
        base[pair, 2] = root * math.sin(turned)
        base[pair, 4] = 0.0 if pair == 0 else 1.0

    part = (chips, planes, full_y, full_z)
    group = [
        wide(16, full_z),
        wide(2, planes, full_y, full_z),
        wide(2, planes - 1, full_y, full_z),
        wide(2, full_y, full_z),
        wide(nodes, 4, rows, full_z),
    ]
    started = pl.pallas_call(
        functools.partial(start_kernel, geometry),
        out_shape=tuple([wide(planes + 2, full_y, full_z)] + group * per_core),
        in_specs=[smem, smem] + [vmem] * 7,
        out_specs=(vmem,) * (1 + 5 * per_core),
        scratch_shapes=[
            held(*part),
            held(*part),
            held(per_core, 2, planes, full_y, full_z),
            held(full_y, full_z),
            held(full_y, full_z),
            held(8, full_z),
            held(space, 8, full_z),
            dma((chips, planes)),
            dma((chips, planes)),
            dma((chips, planes)),
            dma((chips, planes)),
            dma((2,)),
            dma((2,)),
            dma((space,)),
            dma((space,)),
        ],
        compiler_params=params(0),
        name="start",
    )(
        to_pairs,
        coef_first,
        base,
        source,
        initial,
        diffusivity,
        tables.y_forward,
        tables.z_forward,
        tables.lam,
    )
    kappa = started[0]
    solved = []
    for pair in range(per_core):
        sc, rhs, inner, edge, sent = started[1 + 5 * pair : 6 + 5 * pair]
        (got,) = exchange(False, geometry, sc, sent, tables)
        pre_one, out_one, dots, inner, edge, sent = apply_back(
            False, sc, inner, edge, got, tables, kappa, rhs
        )
        got, sc = exchange(True, geometry, sc, sent, tables, (dots,))
        pre_two, dots = apply_back(
            True, sc, inner, edge, got, tables, kappa, rhs, (pre_one, out_one)
        )
        solved += [sc, pre_one, pre_two, dots]
    return pl.pallas_call(
        functools.partial(finish_kernel, geometry),
        out_shape=wide(1, slab, full_y, full_z),
        in_specs=[smem] + [vmem] * len(solved),
        out_specs=vmem,
        scratch_shapes=[
            held(planes, 2 * per_core, full_y, full_z),
            held(planes, 2 * per_core, full_y, full_z),
            held(*part),
            held(per_core, 16, full_z),
            held(per_core, nodes, 16, full_z),
            dma((per_core, nodes)),
            dma((per_core, nodes)),
            dma((planes,)),
            dma((planes,)),
            dma((chips, planes)),
            dma((chips, planes)),
        ],
        compiler_params=params(3),
        name="finish",
    )(from_pairs, *solved)


def solution(mesh):
    cores = 2
    steps = mesh.shape["tm"]
    split = Mesh(
        mesh.devices.reshape(steps // cores, cores, mesh.shape["space"]), ("x", "core", "space")
    )
    in_specs = (P(("x", "core"), "space"), P("space"), P("space"))
    out_specs = P(("x", "core"), "space")
    return jax.shard_map(
        functools.partial(shards, cores),
        mesh=split,
        in_specs=in_specs,
        out_specs=out_specs,
        check_vma=False,
    )
```

```python
import functools
import math

import jax
import jax.numpy as jnp
import ml_dtypes
import numpy as np
from jax import lax
from jax.experimental import pallas as pl
from jax.experimental.pallas import tpu as pltpu
from jax.sharding import Mesh, PartitionSpec as P

alpha_corner = 0.05
step_length = 1.0
vmem_bytes = 56 * 1024 * 1024


def real_basis(length):
    place = np.arange(length)
    angle = 2.0 * np.pi * ((place[:, None] * place[None, :]) % length) / length
    basis = np.where(place[None, :] <= length // 2, np.cos(angle), np.sin(angle))
    return basis / np.sqrt(np.sum(basis * basis, axis=0, keepdims=True))


def wave_symbol(length):
    return 4.0 * np.sin(np.pi * np.arange(length) / length) ** 2


def split_table(table, axis, order):
    high = table.astype(ml_dtypes.bfloat16)
    low = (table - high.astype(np.float64)).astype(ml_dtypes.bfloat16)
    return np.concatenate([high if part == "h" else low for part in order], axis=axis)


def sine_basis(count):
    place = np.arange(1, count + 1)
    return np.sqrt(2.0 / (count + 1)) * np.sin(np.pi * np.outer(place, place) / (count + 1))


def sine_symbol(count):
    return 4.0 * np.sin(np.pi * np.arange(1, count + 1) / (2 * (count + 1))) ** 2


def weighted(factors, values):
    total = None
    for factor, value in zip(factors, values):
        term = float(factor) * value
        total = term if total is None else total + term
    return total


def sine_apply(basis, values):
    count = len(values)
    half = count // 2
    even = [values[j] + values[count - 1 - j] for j in range(half)]
    odd = [values[j] - values[count - 1 - j] for j in range(half)]
    if count % 2:
        even.append(values[half])
    return [
        weighted(basis[k, : len(even)], even) if k % 2 == 0 else weighted(basis[k, :half], odd)
        for k in range(count)
    ]


def halves(values):
    high = values.astype(jnp.bfloat16)
    return high, (values - high.astype(jnp.float32)).astype(jnp.bfloat16)


def left_multiply(table, values):
    high, low = halves(values)
    return jnp.dot(
        table, jnp.concatenate([high, high, low], axis=0), preferred_element_type=jnp.float32
    )


def right_multiply(values, table):
    high, low = halves(values)
    return jnp.dot(
        jnp.concatenate([high, low, high], axis=1), table, preferred_element_type=jnp.float32
    )


def inverse_factors(scalars, symbol):
    shift_a, shift_b, shift_i, mean = scalars[:4]
    diag_a = shift_a + mean * symbol
    diag_b = shift_b + mean * symbol
    scale_a = 1.0 / (diag_a * diag_a + shift_i * shift_i)
    scale_b = 1.0 / (diag_b * diag_b + shift_i * shift_i)
    return diag_a * scale_a, diag_b * scale_b, shift_i * scale_a


def scaled(factors, first, second):
    return (factors[0] * first + factors[2] * second, factors[1] * second - factors[2] * first)


def row(ref, number):
    return ref[pl.ds(number, 1), :]


def transform_plane(first, second, table_y, table_z, work, index):
    full_y, full_z = first.shape
    both = jnp.concatenate([first, second], axis=1)
    both = left_multiply(table_y[...], both)
    both = jnp.concatenate([both[:, :full_z], both[:, full_z:]], axis=0)
    both = right_multiply(both, table_z[...])
    work[0, index] = both[:full_y]
    work[1, index] = both[full_y:]


def loop(start, stop, body):
    def step(index, carry):
        body(index)
        return carry

    lax.fori_loop(start, stop, step, 0)


def remote(src, dst, send, recv, **where):
    return pltpu.make_async_remote_copy(
        src_ref=src,
        dst_ref=dst,
        send_sem=send,
        recv_sem=recv,
        device_id=where,
        device_id_type=pl.DeviceIdType.MESH,
    )


def greet(barrier, **where):
    pl.semaphore_signal(
        barrier, inc=1, device_id=where, device_id_type=pl.DeviceIdType.MESH
    )


def node_place(node, chips):
    return {"space": lax.div(node, chips), "x": lax.rem(node, chips)}


def dot_rows(tiles, nodes, count):
    total = tiles[0]
    for node in range(1, nodes):
        total = total + tiles[node]
    total = jnp.sum(total, axis=1, keepdims=True)
    return [
        jnp.broadcast_to(total[number : number + 1], (1, tiles.shape[2]))
        for number in range(count)
    ]


def pair_coefs(sc, tiles, nodes):
    sums = dot_rows(tiles, nodes, 12)
    mixed = row(sc, 4)
    h_i = row(sc, 7)
    top = hermitian(mixed, sums[0], sums[1], sums[2], sums[3])
    length = hermitian(mixed, sums[4], sums[5], sums[4], sums[4])
    diag = hermitian(mixed, sums[6], sums[7], sums[8], sums[9])
    left = hermitian(mixed, sums[10], sums[11], sums[10], sums[10])
    coefs = []
    for which in range(2):
        h_r, norm2, left2 = row(sc, 5 + which), row(sc, 8 + which), left[which]
        root = jnp.sqrt(norm2) * jnp.sqrt(left2)
        c1, c2 = small_solve(
            norm2,
            (h_r, h_i),
            left2 / norm2,
            [part / root for part in (top[which], top[2])],
            [part / left2 for part in (diag[which], diag[2])],
            length[which] / left2,
        )
        scale_one, scale_two = 1.0 / jnp.sqrt(norm2), 1.0 / jnp.sqrt(left2)
        coefs.append((c1[0] * scale_one, c1[1] * scale_one, c2[0] * scale_two, c2[1] * scale_two))
    return coefs


def turn(values, amount, axis):
    return pltpu.roll(values, amount % values.shape[axis], axis)


def folded(values):
    return jnp.sum(values.reshape(-1, 8, values.shape[-1]), axis=0)


def hermitian(mixed, d00, d11, d01, d10):
    return d00 + mixed * d11, d11 + mixed * d00, mixed * (d01 - d10)


def small_solve(norm2, h11, h21_2, h12, h22, gram_second):
    gram_first = h11[0] * h11[0] + h11[1] * h11[1] + h21_2
    sub = jnp.sqrt(h21_2)
    cross_real = h11[0] * h12[0] + h11[1] * h12[1] + sub * h22[0]
    cross_imag = h11[0] * h12[1] - h11[1] * h12[0] + sub * h22[1]
    norm = jnp.sqrt(norm2)
    one = (norm * h11[0], -norm * h11[1])
    two = (norm * h12[0], -norm * h12[1])
    det = gram_first * gram_second - (cross_real * cross_real + cross_imag * cross_imag)
    c1 = (
        (gram_second * one[0] - (cross_real * two[0] - cross_imag * two[1])) / det,
        (gram_second * one[1] - (cross_real * two[1] + cross_imag * two[0])) / det,
    )
    c2 = (
        (gram_first * two[0] - (cross_real * one[0] + cross_imag * one[1])) / det,
        (gram_first * two[1] - (cross_real * one[1] - cross_imag * one[0])) / det,
    )
    return c1, c2


def window_kernel(
    geometry,
    coef_to,
    coef_first,
    coef_from,
    waves,
    table,
    base,
    source,
    initial,
    diffusivity,
    forward_y,
    forward_z,
    back_y,
    back_z,
    lam,
    out,
    *scratch,
):
    chips, space, per_core = geometry
    (
        opening, dif, mine, other, low, high, share_tile, share_tiles, kappa, sc_all, rhs_all,
        work, work_back, inner, edge, sent_all, got_all, back_all, res_all, spec, known,
        pre_all, out_one, dots, tile_all, tiles_all, sol, twin_sol, fields,
    ) = scratch[:29]
    (
        local, send_x, recv_x, send_c, recv_c, send_h, recv_h, send_m, recv_m,
        send_o, recv_o, send_b, recv_b, send_t, recv_t, send_s, recv_s, send_f, recv_f,
    ) = scratch[29:]
    cores = 2
    nodes = space * chips
    slab, full_y, full_z = dif.shape
    planes = slab // chips
    count = planes - 1
    rows = full_y // nodes
    per_node = waves.shape[1]
    basis, symbol = sine_basis(count), sine_symbol(count)
    chip, core, place = lax.axis_index("x"), lax.axis_index("core"), lax.axis_index("space")
    twin = cores - 1 - core
    position = place * chips + chip
    first = chip * planes

    def node_at(j):
        return lax.rem(position + j, nodes)

    loads = [
        pltpu.make_async_copy(diffusivity, dif, local.at[0]),
        pltpu.make_async_copy(initial.at[pl.ds(first, planes)], opening, local.at[1]),
        pltpu.make_async_copy(source.at[0, pl.ds(first, planes)], mine.at[chip], local.at[2]),
    ]
    for load in loads:
        load.start()

    barrier = pltpu.get_barrier_semaphore()
    loop(1, nodes, lambda j: greet(barrier, **node_place(node_at(j), chips)))
    greet(barrier, core=twin)
    pl.semaphore_wait(barrier, nodes)

    def to_chip(j, index):
        peer = lax.rem(chip + j, chips)
        return remote(
            source.at[0, peer * planes + index],
            mine.at[chip, index],
            send_x.at[j, index],
            recv_x.at[j, index],
            x=peer,
        )

    def own_to_core(index):
        return remote(
            source.at[0, first + index],
            other.at[chip, index],
            send_c.at[0, index],
            recv_c.at[0, index],
            core=twin,
        )

    def to_core(j, index):
        sender = lax.rem(chip + chips - j, chips)
        return remote(
            mine.at[sender, index],
            other.at[sender, index],
            send_c.at[j, index],
            recv_c.at[j, index],
            core=twin,
        )

    def begin(index):
        for j in range(1, chips):
            to_chip(j, index).start()

    loop(0, planes, begin)
    loop(0, planes, lambda index: own_to_core(index).start())
    loads[0].wait()
    after, before = lax.rem(place + 1, space), lax.rem(place + space - 1, space)
    up = remote(dif.at[slab - 1], low, send_h.at[0], recv_h.at[0], space=after)
    down = remote(dif.at[0], high, send_h.at[1], recv_h.at[1], space=before)
    up.start()
    down.start()
    share_tile[...] = jnp.zeros_like(share_tile)

    def add_plane(index):
        share_tile[...] += folded(dif[index])

    loop(0, slab, add_plane)
    shares = [
        remote(
            share_tile,
            share_tiles.at[place],
            send_m.at[j],
            recv_m.at[j],
            space=lax.rem(place + j, space),
        )
        for j in range(1, space)
    ]
    for share in shares:
        share.start()
    share_tiles[place] = share_tile[...]
    loads[1].wait()
    loads[2].wait()

    def relay(index):
        for j in range(1, chips):
            to_chip(j, index).wait_recv()
            to_core(j, index).start()

    def process(index):
        own_to_core(index).wait_recv()
        for j in range(1, chips):
            to_core(j, index).wait_recv()
        for i in range(per_core):
            values = []
            for c in range(2):
                column = (core * per_core + i) * 2 + c
                total = coef_first[0, column] * opening[index]
                for n in range(chips):
                    total = total + coef_to[n * cores + core, column] * mine[n, index]
                    total = total + coef_to[n * cores + twin, column] * other[n, index]
                rhs_all[i, c, index] = total
                values.append(total)
            transform_plane(values[0], values[1], forward_y, forward_z, work.at[i], index)

    relay(0)

    def relay_and_process(index):
        relay(index + 1)
        process(index)

    loop(0, planes - 1, relay_and_process)
    process(planes - 1)

    for share in shares:
        share.wait_recv()
    total = share_tiles[0]
    for j in range(1, space):
        total = total + share_tiles[j]
    total = jnp.sum(jnp.sum(total, axis=0, keepdims=True), axis=1, keepdims=True)
    cells = slab * space * full_y * full_z
    for i in range(per_core):
        sc_all[i] = base[core * per_core + i]
        sc_all[i, pl.ds(3, 1)] = jnp.broadcast_to(total / cells, (1, full_z))

    def out_to(phase, j):
        peer = node_at(j)
        return remote(
            sent_all.at[phase, peer],
            got_all.at[phase, position],
            send_o.at[phase, j],
            recv_o.at[phase, j],
            **node_place(peer, chips),
        )

    def home_to(phase, j):
        peer = node_at(j)
        return remote(
            back_all.at[phase, peer],
            res_all.at[phase, position],
            send_b.at[phase, j],
            recv_b.at[phase, j],
            **node_place(peer, chips),
        )

    def dots_to(phase, j):
        return remote(
            tile_all.at[phase],
            tiles_all.at[phase, position],
            send_t.at[phase, j],
            recv_t.at[phase, j],
            **node_place(node_at(j), chips),
        )

    def share_dots(phase, number_of):
        tile = tile_all.at[phase]
        tile[...] = jnp.zeros(tile.shape, jnp.float32)
        for number in range(number_of):
            tile[pl.ds(number, 1), :] = jnp.sum(dots[number], axis=0, keepdims=True)
        loop(1, nodes, lambda j: dots_to(phase, j).start())
        tiles_all[phase, position] = tile[...]

    def inner_solve(pair, phase):
        sc, spectrum = sc_all.at[pair], work.at[pair]
        sent = sent_all.at[phase]
        scalars = [row(sc, number) for number in range(4)]
        mean = scalars[3]

        def chunk(index):
            rng = pl.ds(pl.multiple_of(index * rows, rows), rows)
            values = [
                sine_apply(basis, [spectrum[c, j, rng] for j in range(count)]) for c in range(2)
            ]
            ends = [[None, None], [None, None]]
            for k in range(count):
                factors = inverse_factors(scalars, lam[rng] + float(symbol[k]))
                for c, value in enumerate(scaled(factors, values[0][k], values[1][k])):
                    inner[c, k, rng] = value
                    for end, at in ((0, 0), (1, count - 1)):
                        term = float(basis[at, k]) * value
                        ends[c][end] = term if k == 0 else ends[c][end] + term
            for c in range(2):
                own = spectrum[c, count, rng]
                edge[c, rng] = own
                sent[index, c] = own + mean * ends[c][1]
                sent[index, 2 + c] = mean * ends[c][0]

        def send(j):
            chunk(node_at(j))
            out_to(phase, j).start()

        loop(1, nodes, send)
        chunk(position)

    def exchange(pair, phase, second):
        sc, got, back = sc_all.at[pair], got_all.at[phase], back_all.at[phase]
        scalars = [row(sc, number) for number in range(4)]
        if not second:
            lam_value = lam[pl.ds(pl.multiple_of(position * rows, rows), rows)]

            def know(mode):
                factors = None
                for part in range(per_node):
                    term = inverse_factors(scalars, lam_value + waves[mode, part])
                    factors = term if factors is None else [a + b for a, b in zip(factors, term)]
                for number in range(3):
                    known[mode, number] = factors[number] * (1.0 / per_node)

            loop(0, nodes, know)
        got[position] = sent_all[phase, position]
        loop(1, nodes, lambda j: out_to(phase, j).wait_recv())

        def to_modes(mode):
            values = []
            for c in range(2):
                total = None
                for d in range(nodes):
                    term = table[d, mode] * (got[d, c] + got[(d + 1) % nodes, 2 + c])
                    total = term if total is None else total + term
                values.append(total)
            factors = [known[mode, number] for number in range(3)]
            spec[mode, 0], spec[mode, 1] = scaled(factors, values[0], values[1])

        loop(0, nodes, to_modes)

        def from_modes(j):
            node = node_at(j)
            following = node_at(j + 1)
            for c in range(2):
                total = None
                for mode in range(nodes):
                    term = table[node, mode] * spec[mode, c]
                    total = term if total is None else total + term
                back[node, c] = total
                back[following, 2 + c] = total

        from_modes(0)

        def send_home(j):
            from_modes(j)
            home_to(phase, j).start()

        loop(1, nodes, send_home)
        res_all[phase, position] = back[position]

    def first_sums(pair, phase):
        sc = sc_all.at[pair]
        loop(1, nodes, lambda j: dots_to(phase, j).wait_recv())
        sums = dot_rows(tiles_all.at[phase], nodes, 8)
        mixed = row(sc, 4)
        norm_a, norm_b, _ = hermitian(mixed, sums[6], sums[7], sums[6], sums[6])
        top = hermitian(mixed, sums[0], sums[1], sums[2], sums[3])
        values = (top[0] / norm_a, top[1] / norm_b, top[2] / norm_a, norm_a, norm_b)
        for number, value in enumerate(values):
            sc[pl.ds(5 + number, 1), :] = value

    def operate(pair, phase, second):
        sc, res, rhs = sc_all.at[pair], res_all.at[phase], rhs_all.at[pair]
        pre = pre_all.at[phase]
        prior = pre_all.at[2 * pair]
        scalars = [row(sc, number) for number in range(4)]
        shift_a, shift_b, shift_i, mean = scalars
        if second:
            h_a, h_b, h_i = [row(sc, number) for number in range(5, 8)]

        def chunk(index):
            rng = pl.ds(pl.multiple_of(index * rows, rows), rows)
            own = [res[index, c] for c in range(2)]
            left = [res[index, 2 + c] for c in range(2)]
            lam_value = lam[rng]
            values = [[], []]
            for k in range(count):
                factors = inverse_factors(scalars, lam_value + float(symbol[k]))
                ends = [
                    mean * (float(basis[0, k]) * left[c] + float(basis[count - 1, k]) * own[c])
                    for c in range(2)
                ]
                for c, value in enumerate(scaled(factors, ends[0], ends[1])):
                    values[c].append(inner[c, k, rng] + value)
            diag = mean * (lam_value + 2.0)
            lifted = (
                (shift_a + diag) * own[0] - shift_i * own[1],
                (shift_b + diag) * own[1] + shift_i * own[0],
            )
            for c in range(2):
                solved = sine_apply(basis, values[c])
                for j in range(count):
                    work_back[c, 1 + j, rng] = solved[j]
                work_back[c, 0, rng] = left[c]
                work_back[c, planes, rng] = own[c]
                work_back[c, planes + 1, rng] = (lifted[c] - edge[c, rng]) / mean - solved[-1]

        chunk(position)

        def arrived(j):
            home_to(phase, j).wait_recv()
            chunk(lax.rem(position + nodes - j, nodes))

        loop(1, nodes, arrived)

        def to_cells(index):
            both = jnp.concatenate([work_back[0, index], work_back[1, index]], axis=0)
            both = right_multiply(both, back_z[...])
            both = jnp.concatenate([both[:full_y], both[full_y:]], axis=1)
            both = left_multiply(back_y[...], both)
            value = [both[:, :full_z], both[:, full_z:]]
            if second:
                old = [prior[0, index], prior[1, index]]
                value = [
                    value[0] - (h_a * old[0] - h_i * old[1]),
                    value[1] - (h_b * old[1] + h_i * old[0]),
                ]
            pre[0, index] = value[0]
            pre[1, index] = value[1]

        def stencil(index):
            mid = kappa[index + 1]
            face_after = 0.5 * (mid + kappa[index + 2])
            face_before = 0.5 * (mid + kappa[index])
            face_y = 0.5 * (mid + turn(mid, -1, 0))
            face_z = 0.5 * (mid + turn(mid, -1, 1))
            here = [pre[c, index + 1] for c in range(2)]
            result = []
            for c in range(2):
                total = face_after * (here[c] - pre[c, index + 2])
                total = total + face_before * (here[c] - pre[c, index])
                flux = face_y * (here[c] - turn(here[c], -1, 0))
                total = total + (flux - turn(flux, 1, 0))
                flux = face_z * (here[c] - turn(here[c], -1, 1))
                total = total + (flux - turn(flux, 1, 1))
                result.append(step_length * total)
            result[0] = result[0] + (shift_a * here[0] - shift_i * here[1])
            result[1] = result[1] + (shift_b * here[1] + shift_i * here[0])
            start = [rhs[0, index], rhs[1, index]]
            pairs = [(start[0], result[0]), (start[1], result[1])]
            pairs += [(start[0], result[1]), (start[1], result[0])]
            pairs += [(result[0], result[0]), (result[1], result[1])]
            if second:
                old = [out_one[0, index], out_one[1, index]]
                rest_a = old[0] - (h_a * start[0] - h_i * start[1])
                rest_b = old[1] - (h_b * start[1] + h_i * start[0])
                pairs += [(rest_a, result[0]), (rest_b, result[1])]
                pairs += [(rest_a, result[1]), (rest_b, result[0])]
                pairs += [(rest_a, rest_a), (rest_b, rest_b)]
            else:
                out_one[0, index] = result[0]
                out_one[1, index] = result[1]
                transform_plane(
                    result[0], result[1], forward_y, forward_z, work.at[pair], index
                )
                pairs += [(start[0], start[0]), (start[1], start[1])]
            for number, (one, two) in enumerate(pairs):
                dots[number] += folded(one * two)

        dots[...] = jnp.zeros_like(dots)
        ahead = min(3, planes + 2)
        loop(0, ahead, to_cells)

        def both(index):
            stencil(index)
            to_cells(index + ahead)

        loop(0, planes + 2 - ahead, both)
        loop(planes + 2 - ahead, planes, stencil)
        share_dots(phase, 12 if second else 8)

    for pair in range(per_core):
        inner_solve(pair, 2 * pair)
        if pair == 0:
            up.wait_recv()
            down.wait_recv()
            kappa[0] = jnp.where(chip > 0, dif[jnp.maximum(first - 1, 0)], low[...])
            kappa[planes + 1] = jnp.where(
                chip < chips - 1, dif[jnp.minimum(first + planes, slab - 1)], high[...]
            )

            def keep_kappa(index):
                kappa[index + 1] = dif[first + index]

            loop(0, planes, keep_kappa)
        exchange(pair, 2 * pair, False)
        operate(pair, 2 * pair, False)
        inner_solve(pair, 2 * pair + 1)
        first_sums(pair, 2 * pair)
        exchange(pair, 2 * pair + 1, True)
        operate(pair, 2 * pair + 1, True)

    coefs = []
    for pair in range(per_core):
        loop(1, nodes, lambda j: dots_to(2 * pair + 1, j).wait_recv())
        coefs.append(pair_coefs(sc_all.at[pair], tiles_all.at[2 * pair + 1], nodes))

    def sol_to_core(index):
        return remote(
            sol.at[index], twin_sol.at[index], send_s.at[index], recv_s.at[index], core=twin
        )

    def field_to_chip(j, index):
        peer = lax.rem(chip + j, chips)
        return remote(
            fields.at[peer, index],
            out.at[0, first + index],
            send_f.at[j, index],
            recv_f.at[j, index],
            x=peer,
        )

    def combine(index):
        for i in range(per_core):
            ca, cb = coefs[i]
            one = [pre_all[2 * i, c, index + 1] for c in range(2)]
            two = [pre_all[2 * i + 1, c, index + 1] for c in range(2)]
            sol[index, 2 * i] = ca[0] * one[0] - ca[1] * one[1] + ca[2] * two[0] - ca[3] * two[1]
            sol[index, 2 * i + 1] = (
                cb[0] * one[1] + cb[1] * one[0] + cb[2] * two[1] + cb[3] * two[0]
            )
        sol_to_core(index).start()

    def spread(index):
        sol_to_core(index).wait_recv()

        def field(peer):
            total = None
            for part in range(2 * per_core):
                own = coef_from[peer * cores + core, core * per_core * 2 + part]
                far = coef_from[peer * cores + core, twin * per_core * 2 + part]
                term = own * sol[index, part] + far * twin_sol[index, part]
                total = term if total is None else total + term
            return total

        for j in range(1, chips):
            peer = lax.rem(chip + j, chips)
            fields[peer, index] = field(peer)
            field_to_chip(j, index).start()
        out[0, first + index] = field(chip)

    combine(0)

    def combine_and_spread(index):
        combine(index + 1)
        spread(index)

    loop(0, planes - 1, combine_and_spread)
    spread(planes - 1)

    up.wait_send()
    down.wait_send()
    for share in shares:
        share.wait_send()

    def end(index):
        own_to_core(index).wait_send()
        sol_to_core(index).wait_send()
        for j in range(1, chips):
            to_chip(j, index).wait_send()
            to_core(j, index).wait_send()

    def end_node(j):
        for phase in range(2 * per_core):
            out_to(phase, j).wait_send()
            home_to(phase, j).wait_send()
            dots_to(phase, j).wait_send()

    def end_fields(index):
        for j in range(1, chips):
            field_to_chip(j, index).wait_send()
            field_to_chip(j, index).wait_recv()

    loop(0, planes, end)
    loop(1, nodes, end_node)
    loop(0, planes, end_fields)


smem = pl.BlockSpec(memory_space=pltpu.SMEM)
vmem = pl.BlockSpec(memory_space=pltpu.VMEM)
anywhere = pl.BlockSpec(memory_space=pl.ANY)
dma = pltpu.SemaphoreType.DMA


def held(*shape):
    return pltpu.VMEM(shape, jnp.float32)


class Tables:
    def __init__(self, full_x, full_y, full_z, nodes):
        basis_y, basis_z = real_basis(full_y), real_basis(full_z)
        self.y_forward = split_table(basis_y.T, 1, "hlh")
        self.y_back = split_table(basis_y, 1, "hlh")
        self.z_forward = split_table(basis_z, 0, "hhl")
        self.z_back = split_table(basis_z.T, 0, "hhl")
        lam = wave_symbol(full_y)[:, None] + wave_symbol(full_z)[None, :]
        self.lam = lam.astype(np.float32)
        self.nodes = nodes
        waves = wave_symbol(full_x).reshape(full_x // nodes, nodes).T
        self.waves = np.ascontiguousarray(waves).astype(np.float32)
        self.over_nodes = real_basis(nodes).astype(np.float32)


def shards(cores, source, initial, diffusivity):
    chips = lax.axis_size("x")
    steps = chips * cores
    space = lax.axis_size("space")
    nodes = space * chips
    slab, full_y, full_z = diffusivity.shape
    planes = slab // chips
    full_x = slab * space
    rows = full_y // nodes
    tables = Tables(full_x, full_y, full_z, nodes)

    pairs = steps // 2
    per_core = pairs // cores
    geometry = (chips, space, per_core)
    angle = 2.0 * np.pi * np.outer(np.arange(steps), np.arange(pairs)) / steps
    to_pairs = np.stack([np.cos(angle), -np.sin(angle)], axis=2)
    to_pairs[:, 0, 1] = (-1.0) ** np.arange(steps)
    from_pairs = 2.0 * to_pairs / steps
    from_pairs[:, 0] = to_pairs[:, 0] / steps
    decay = (alpha_corner ** (np.arange(steps) / steps))[:, None]
    to_pairs = to_pairs.reshape(steps, steps)
    coef_first = to_pairs[:1].astype(np.float32)
    to_pairs = (to_pairs * decay * step_length).astype(np.float32)
    from_pairs = (from_pairs.reshape(steps, steps) / decay).astype(np.float32)
    root = alpha_corner ** (1.0 / steps)
    base = np.zeros((pairs, 16, full_z), np.float32)
    for pair in range(pairs):
        turned = 2.0 * math.pi * pair / steps
        base[pair, 0] = 1.0 - root * math.cos(turned)
        base[pair, 1] = 1.0 + root if pair == 0 else base[pair, 0]
        base[pair, 2] = root * math.sin(turned)
        base[pair, 4] = 0.0 if pair == 0 else 1.0

    plane = (full_y, full_z)
    phases = 2 * per_core
    message = (phases, nodes, 4, rows, full_z)
    by_plane, by_node = dma((chips, planes)), dma((phases, nodes))
    return pl.pallas_call(
        functools.partial(window_kernel, geometry),
        out_shape=jax.ShapeDtypeStruct((1, slab, full_y, full_z), jnp.float32),
        in_specs=[smem] * 5 + [vmem] + [anywhere] * 3 + [vmem] * 5,
        out_specs=vmem,
        scratch_shapes=[
            held(planes, *plane),
            held(slab, *plane),
            held(chips, planes, *plane),
            held(chips, planes, *plane),
            held(*plane),
            held(*plane),
            held(8, full_z),
            held(space, 8, full_z),
            held(planes + 2, *plane),
            held(per_core, 16, full_z),
            held(per_core, 2, planes, *plane),
            held(per_core, 2, planes, *plane),
            held(2, planes + 2, *plane),
            held(2, planes - 1, *plane),
            held(2, *plane),
            held(*message),
            held(*message),
            held(*message),
            held(*message),
            held(nodes, 2, rows, full_z),
            held(nodes, 3, rows, full_z),
            held(phases, 2, planes + 2, *plane),
            held(2, planes, *plane),
            held(12, 8, full_z),
            held(phases, 16, full_z),
            held(phases, nodes, 16, full_z),
            held(planes, phases, *plane),
            held(planes, phases, *plane),
            held(chips, planes, *plane),
            dma((3,)),
            by_plane,
            by_plane,
            by_plane,
            by_plane,
            dma((2,)),
            dma((2,)),
            dma((space,)),
            dma((space,)),
            by_node,
            by_node,
            by_node,
            by_node,
            by_node,
            by_node,
            dma((planes,)),
            dma((planes,)),
            by_plane,
            by_plane,
        ],
        compiler_params=pltpu.CompilerParams(
            vmem_limit_bytes=vmem_bytes, collective_id=0, has_side_effects=True
        ),
        name="window",
    )(
        to_pairs,
        coef_first,
        from_pairs,
        tables.waves,
        tables.over_nodes,
        base,
        source,
        initial,
        diffusivity,
        tables.y_forward,
        tables.z_forward,
        tables.y_back,
        tables.z_back,
        tables.lam,
    )


def solution(mesh):
    cores = 2
    steps = mesh.shape["tm"]
    split = Mesh(
        mesh.devices.reshape(steps // cores, cores, mesh.shape["space"]), ("x", "core", "space")
    )
    in_specs = (P(("x", "core"), "space"), P("space"), P("space"))
    out_specs = P(("x", "core"), "space")
    return jax.shard_map(
        functools.partial(shards, cores),
        mesh=split,
        in_specs=in_specs,
        out_specs=out_specs,
        check_vma=False,
    )
```

```python
import functools
import math

import jax
import jax.numpy as jnp
import ml_dtypes
import numpy as np
from jax import lax
from jax.experimental import pallas as pl
from jax.experimental.pallas import tpu as pltpu
from jax.sharding import Mesh, PartitionSpec as P

alpha_corner = 0.05
step_length = 1.0
vmem_bytes = 56 * 1024 * 1024


def real_basis(length):
    place = np.arange(length)
    angle = 2.0 * np.pi * ((place[:, None] * place[None, :]) % length) / length
    basis = np.where(place[None, :] <= length // 2, np.cos(angle), np.sin(angle))
    return basis / np.sqrt(np.sum(basis * basis, axis=0, keepdims=True))


def wave_symbol(length):
    return 4.0 * np.sin(np.pi * np.arange(length) / length) ** 2


def split_table(table, axis, order):
    high = table.astype(ml_dtypes.bfloat16)
    low = (table - high.astype(np.float64)).astype(ml_dtypes.bfloat16)
    return np.concatenate([high if part == "h" else low for part in order], axis=axis)


def sine_basis(count):
    place = np.arange(1, count + 1)
    return np.sqrt(2.0 / (count + 1)) * np.sin(np.pi * np.outer(place, place) / (count + 1))


def sine_symbol(count):
    return 4.0 * np.sin(np.pi * np.arange(1, count + 1) / (2 * (count + 1))) ** 2


def weighted(factors, values):
    total = None
    for factor, value in zip(factors, values):
        term = float(factor) * value
        total = term if total is None else total + term
    return total


def sine_apply(basis, values):
    count = len(values)
    half = count // 2
    even = [values[j] + values[count - 1 - j] for j in range(half)]
    odd = [values[j] - values[count - 1 - j] for j in range(half)]
    if count % 2:
        even.append(values[half])
    return [
        weighted(basis[k, : len(even)], even) if k % 2 == 0 else weighted(basis[k, :half], odd)
        for k in range(count)
    ]


def halves(values):
    high = values.astype(jnp.bfloat16)
    return high, (values - high.astype(jnp.float32)).astype(jnp.bfloat16)


def left_multiply(table, values):
    high, low = halves(values)
    return jnp.dot(
        table, jnp.concatenate([high, high, low], axis=0), preferred_element_type=jnp.float32
    )


def right_multiply(values, table):
    high, low = halves(values)
    return jnp.dot(
        jnp.concatenate([high, low, high], axis=1), table, preferred_element_type=jnp.float32
    )


def inverse_factors(scalars, symbol):
    shift_a, shift_b, shift_i, mean = scalars[:4]
    diag_a = shift_a + mean * symbol
    diag_b = shift_b + mean * symbol
    scale_a = 1.0 / (diag_a * diag_a + shift_i * shift_i)
    scale_b = 1.0 / (diag_b * diag_b + shift_i * shift_i)
    return diag_a * scale_a, diag_b * scale_b, shift_i * scale_a


def scaled(factors, first, second):
    return (factors[0] * first + factors[2] * second, factors[1] * second - factors[2] * first)


def row(ref, number):
    return ref[pl.ds(number, 1), :]


def transform_plane(first, second, table_y, work, index):
    full_z = first.shape[1]
    both = left_multiply(table_y[...], jnp.concatenate([first, second], axis=1))
    work[0, index] = both[:, :full_z]
    work[1, index] = both[:, full_z:]


def transform_rows(groups, table_z):
    rows = groups[0][0].shape[0]
    stacked = jnp.concatenate([value for group in groups for value in group], axis=0)
    stacked = right_multiply(stacked, table_z[...])
    values = [stacked[n * rows : (n + 1) * rows] for n in range(stacked.shape[0] // rows)]
    size = len(groups[0])
    return [values[c * size : (c + 1) * size] for c in range(len(groups))]


def loop(start, stop, body):
    def step(index, carry):
        body(index)
        return carry

    lax.fori_loop(start, stop, step, 0)


def remote(src, dst, send, recv, **where):
    return pltpu.make_async_remote_copy(
        src_ref=src,
        dst_ref=dst,
        send_sem=send,
        recv_sem=recv,
        device_id=where,
        device_id_type=pl.DeviceIdType.MESH,
    )


def greet(barrier, **where):
    pl.semaphore_signal(
        barrier, inc=1, device_id=where, device_id_type=pl.DeviceIdType.MESH
    )


def node_place(node, chips):
    return {"space": lax.div(node, chips), "x": lax.rem(node, chips)}


def dot_rows(tiles, nodes, count):
    total = tiles[0]
    for node in range(1, nodes):
        total = total + tiles[node]
    total = jnp.sum(total, axis=1, keepdims=True)
    return [
        jnp.broadcast_to(total[number : number + 1], (1, tiles.shape[2]))
        for number in range(count)
    ]


def pair_coefs(sc, tiles, nodes):
    sums = dot_rows(tiles, nodes, 12)
    mixed = row(sc, 4)
    h_i = row(sc, 7)
    top = hermitian(mixed, sums[0], sums[1], sums[2], sums[3])
    length = hermitian(mixed, sums[4], sums[5], sums[4], sums[4])
    diag = hermitian(mixed, sums[6], sums[7], sums[8], sums[9])
    left = hermitian(mixed, sums[10], sums[11], sums[10], sums[10])
    coefs = []
    for which in range(2):
        h_r, norm2, left2 = row(sc, 5 + which), row(sc, 8 + which), left[which]
        root = jnp.sqrt(norm2) * jnp.sqrt(left2)
        c1, c2 = small_solve(
            norm2,
            (h_r, h_i),
            left2 / norm2,
            [part / root for part in (top[which], top[2])],
            [part / left2 for part in (diag[which], diag[2])],
            length[which] / left2,
        )
        scale_one, scale_two = 1.0 / jnp.sqrt(norm2), 1.0 / jnp.sqrt(left2)
        coefs.append((c1[0] * scale_one, c1[1] * scale_one, c2[0] * scale_two, c2[1] * scale_two))
    return coefs


def turn(values, amount, axis):
    return pltpu.roll(values, amount % values.shape[axis], axis)


def folded(values):
    return jnp.sum(values.reshape(-1, 8, values.shape[-1]), axis=0)


def hermitian(mixed, d00, d11, d01, d10):
    return d00 + mixed * d11, d11 + mixed * d00, mixed * (d01 - d10)


def small_solve(norm2, h11, h21_2, h12, h22, gram_second):
    gram_first = h11[0] * h11[0] + h11[1] * h11[1] + h21_2
    sub = jnp.sqrt(h21_2)
    cross_real = h11[0] * h12[0] + h11[1] * h12[1] + sub * h22[0]
    cross_imag = h11[0] * h12[1] - h11[1] * h12[0] + sub * h22[1]
    norm = jnp.sqrt(norm2)
    one = (norm * h11[0], -norm * h11[1])
    two = (norm * h12[0], -norm * h12[1])
    det = gram_first * gram_second - (cross_real * cross_real + cross_imag * cross_imag)
    c1 = (
        (gram_second * one[0] - (cross_real * two[0] - cross_imag * two[1])) / det,
        (gram_second * one[1] - (cross_real * two[1] + cross_imag * two[0])) / det,
    )
    c2 = (
        (gram_first * two[0] - (cross_real * one[0] + cross_imag * one[1])) / det,
        (gram_first * two[1] - (cross_real * one[1] - cross_imag * one[0])) / det,
    )
    return c1, c2


def window_kernel(
    geometry,
    coef_to,
    coef_first,
    coef_from,
    waves,
    table,
    base,
    source,
    initial,
    diffusivity,
    forward_y,
    forward_z,
    back_y,
    back_z,
    lam,
    out,
    *scratch,
):
    chips, space, per_core = geometry
    (
        opening, dif, mine, other, low, high, share_tile, share_tiles, kappa, sc_all, rhs_all,
        work, work_back, inner, edge, sent_all, got_all, back_all, res_all, spec, known,
        pre_all, out_one, dots, tile_all, tiles_all, sol, twin_sol, fields,
    ) = scratch[:29]
    (
        local, send_x, recv_x, send_c, recv_c, send_h, recv_h, send_m, recv_m,
        send_o, recv_o, send_b, recv_b, send_t, recv_t, send_s, recv_s, send_f, recv_f,
    ) = scratch[29:]
    cores = 2
    nodes = space * chips
    slab, full_y, full_z = dif.shape
    planes = slab // chips
    count = planes - 1
    rows = full_y // nodes
    per_node = waves.shape[1]
    parts, size = sent_all.shape[1], sent_all.shape[4]
    basis, symbol = sine_basis(count), sine_symbol(count)
    chip, core, place = lax.axis_index("x"), lax.axis_index("core"), lax.axis_index("space")
    twin = cores - 1 - core
    position = place * chips + chip
    first = chip * planes

    def node_at(j):
        return lax.rem(position + j, nodes)

    loads = [
        pltpu.make_async_copy(diffusivity, dif, local.at[0]),
        pltpu.make_async_copy(initial.at[pl.ds(first, planes)], opening, local.at[1]),
        pltpu.make_async_copy(source.at[0, pl.ds(first, planes)], mine.at[chip], local.at[2]),
    ]
    for load in loads:
        load.start()

    barrier = pltpu.get_barrier_semaphore()
    loop(1, nodes, lambda j: greet(barrier, **node_place(node_at(j), chips)))
    greet(barrier, core=twin)
    pl.semaphore_wait(barrier, nodes)

    def to_chip(j, index):
        peer = lax.rem(chip + j, chips)
        return remote(
            source.at[0, peer * planes + index],
            mine.at[chip, index],
            send_x.at[j, index],
            recv_x.at[j, index],
            x=peer,
        )

    def own_to_core(index):
        return remote(
            source.at[0, first + index],
            other.at[chip, index],
            send_c.at[0, index],
            recv_c.at[0, index],
            core=twin,
        )

    def to_core(j, index):
        sender = lax.rem(chip + chips - j, chips)
        return remote(
            mine.at[sender, index],
            other.at[sender, index],
            send_c.at[j, index],
            recv_c.at[j, index],
            core=twin,
        )

    def begin(index):
        for j in range(1, chips):
            to_chip(j, index).start()

    loop(0, planes, begin)
    loop(0, planes, lambda index: own_to_core(index).start())
    loads[0].wait()
    after, before = lax.rem(place + 1, space), lax.rem(place + space - 1, space)
    up = remote(dif.at[slab - 1], low, send_h.at[0], recv_h.at[0], space=after)
    down = remote(dif.at[0], high, send_h.at[1], recv_h.at[1], space=before)
    up.start()
    down.start()
    share_tile[...] = jnp.zeros_like(share_tile)

    def add_plane(index):
        share_tile[...] += folded(dif[index])

    loop(0, slab, add_plane)
    shares = [
        remote(
            share_tile,
            share_tiles.at[place],
            send_m.at[j],
            recv_m.at[j],
            space=lax.rem(place + j, space),
        )
        for j in range(1, space)
    ]
    for share in shares:
        share.start()
    share_tiles[place] = share_tile[...]
    loads[1].wait()
    loads[2].wait()

    def relay(index):
        for j in range(1, chips):
            to_chip(j, index).wait_recv()
            to_core(j, index).start()

    def process(index):
        own_to_core(index).wait_recv()
        for j in range(1, chips):
            to_core(j, index).wait_recv()
        for i in range(per_core):
            values = []
            for c in range(2):
                column = (core * per_core + i) * 2 + c
                total = coef_first[0, column] * opening[index]
                for n in range(chips):
                    total = total + coef_to[n * cores + core, column] * mine[n, index]
                    total = total + coef_to[n * cores + twin, column] * other[n, index]
                rhs_all[i, c, index] = total
                values.append(total)
            transform_plane(values[0], values[1], forward_y, work.at[i], index)

    relay(0)

    def relay_and_process(index):
        relay(index + 1)
        process(index)

    loop(0, planes - 1, relay_and_process)
    process(planes - 1)

    for share in shares:
        share.wait_recv()
    total = share_tiles[0]
    for j in range(1, space):
        total = total + share_tiles[j]
    total = jnp.sum(jnp.sum(total, axis=0, keepdims=True), axis=1, keepdims=True)
    cells = slab * space * full_y * full_z
    for i in range(per_core):
        sc_all[i] = base[core * per_core + i]
        sc_all[i, pl.ds(3, 1)] = jnp.broadcast_to(total / cells, (1, full_z))

    def out_to(phase, part, j):
        peer = node_at(j)
        return remote(
            sent_all.at[phase, part, peer],
            got_all.at[phase, part, position],
            send_o.at[phase, part, j],
            recv_o.at[phase, part, j],
            **node_place(peer, chips),
        )

    def home_to(phase, part, j):
        peer = node_at(j)
        return remote(
            back_all.at[phase, part, peer],
            res_all.at[phase, part, position],
            send_b.at[phase, part, j],
            recv_b.at[phase, part, j],
            **node_place(peer, chips),
        )

    def dots_to(phase, j):
        return remote(
            tile_all.at[phase],
            tiles_all.at[phase, position],
            send_t.at[phase, j],
            recv_t.at[phase, j],
            **node_place(node_at(j), chips),
        )

    def share_dots(phase, number_of):
        tile = tile_all.at[phase]
        tile[...] = jnp.zeros(tile.shape, jnp.float32)
        for number in range(number_of):
            tile[pl.ds(number, 1), :] = jnp.sum(dots[number], axis=0, keepdims=True)
        loop(1, nodes, lambda j: dots_to(phase, j).start())
        tiles_all[phase, position] = tile[...]

    def inner_solve(pair, phase):
        sc, spectrum = sc_all.at[pair], work.at[pair]
        sent = sent_all.at[phase]
        scalars = [row(sc, number) for number in range(4)]
        mean = scalars[3]

        def chunk(index):
            rng = pl.ds(pl.multiple_of(index * rows, rows), rows)
            spectral = transform_rows(
                [[spectrum[c, j, rng] for j in range(planes)] for c in range(2)], forward_z
            )
            values = [sine_apply(basis, spectral[c][:count]) for c in range(2)]
            ends = [[None, None], [None, None]]
            for k in range(count):
                factors = inverse_factors(scalars, lam[rng] + float(symbol[k]))
                for c, value in enumerate(scaled(factors, values[0][k], values[1][k])):
                    inner[c, k, rng] = value
                    for end, at in ((0, 0), (1, count - 1)):
                        term = float(basis[at, k]) * value
                        ends[c][end] = term if k == 0 else ends[c][end] + term
            for c in range(2):
                own = spectral[c][count]
                edge[c, rng] = own
                for number, value in ((c, own + mean * ends[c][1]), (2 + c, mean * ends[c][0])):
                    for part in range(parts):
                        sent[part, index, number] = value[part * size : (part + 1) * size]

        def send(j):
            chunk(node_at(j))
            out_to(phase, 0, j).start()

        loop(1, nodes, send)
        for part in range(1, parts):
            loop(1, nodes, lambda j: out_to(phase, part, j).start())
        chunk(position)

    def know(pair):
        scalars = [row(sc_all.at[pair], number) for number in range(4)]
        lam_value = lam[pl.ds(pl.multiple_of(position * rows, rows), rows)]

        def one(mode):
            factors = None
            for part in range(per_node):
                term = inverse_factors(scalars, lam_value + waves[mode, part])
                factors = term if factors is None else [a + b for a, b in zip(factors, term)]
            for number in range(3):
                value = factors[number] * (1.0 / per_node)
                for part in range(parts):
                    known[part, mode, number] = value[part * size : (part + 1) * size]

        loop(0, nodes, one)

    def exchange(phase, part):
        got, back = got_all.at[phase, part], back_all.at[phase, part]
        got[position] = sent_all[phase, part, position]
        loop(1, nodes, lambda j: out_to(phase, part, j).wait_recv())

        def to_modes(mode):
            values = []
            for c in range(2):
                total = None
                for d in range(nodes):
                    term = table[d, mode] * (got[d, c] + got[(d + 1) % nodes, 2 + c])
                    total = term if total is None else total + term
                values.append(total)
            factors = [known[part, mode, number] for number in range(3)]
            spec[mode, 0], spec[mode, 1] = scaled(factors, values[0], values[1])

        loop(0, nodes, to_modes)

        def from_modes(j):
            node = node_at(j)
            following = node_at(j + 1)
            for c in range(2):
                total = None
                for mode in range(nodes):
                    term = table[node, mode] * spec[mode, c]
                    total = term if total is None else total + term
                back[node, c] = total
                back[following, 2 + c] = total

        from_modes(0)

        def send_home(j):
            from_modes(j)
            home_to(phase, part, j).start()

        loop(1, nodes, send_home)
        res_all[phase, part, position] = back[position]

    def first_sums(pair, phase):
        sc = sc_all.at[pair]
        loop(1, nodes, lambda j: dots_to(phase, j).wait_recv())
        sums = dot_rows(tiles_all.at[phase], nodes, 8)
        mixed = row(sc, 4)
        norm_a, norm_b, _ = hermitian(mixed, sums[6], sums[7], sums[6], sums[6])
        top = hermitian(mixed, sums[0], sums[1], sums[2], sums[3])
        values = (top[0] / norm_a, top[1] / norm_b, top[2] / norm_a, norm_a, norm_b)
        for number, value in enumerate(values):
            sc[pl.ds(5 + number, 1), :] = value

    def operate(pair, phase, second):
        sc, res, rhs = sc_all.at[pair], res_all.at[phase], rhs_all.at[pair]
        pre = pre_all.at[phase]
        prior = pre_all.at[2 * pair]
        scalars = [row(sc, number) for number in range(4)]
        shift_a, shift_b, shift_i, mean = scalars
        if second:
            h_a, h_b, h_i = [row(sc, number) for number in range(5, 8)]

        def chunk(index):
            rng = pl.ds(pl.multiple_of(index * rows, rows), rows)
            ends = [
                jnp.concatenate([res[part, index, number] for part in range(parts)], axis=0)
                for number in range(4)
            ]
            own, left = ends[:2], ends[2:]
            lam_value = lam[rng]
            values = [[], []]
            for k in range(count):
                factors = inverse_factors(scalars, lam_value + float(symbol[k]))
                ends = [
                    mean * (float(basis[0, k]) * left[c] + float(basis[count - 1, k]) * own[c])
                    for c in range(2)
                ]
                for c, value in enumerate(scaled(factors, ends[0], ends[1])):
                    values[c].append(inner[c, k, rng] + value)
            diag = mean * (lam_value + 2.0)
            lifted = (
                (shift_a + diag) * own[0] - shift_i * own[1],
                (shift_b + diag) * own[1] + shift_i * own[0],
            )
            lines = []
            for c in range(2):
                solved = sine_apply(basis, values[c])
                beyond = (lifted[c] - edge[c, rng]) / mean - solved[-1]
                lines.append([left[c], *solved, own[c], beyond])
            for c, line in enumerate(transform_rows(lines, back_z)):
                for j, value in enumerate(line):
                    work_back[c, j, rng] = value

        chunk(position)

        def arrived(j):
            for part in range(parts):
                home_to(phase, part, j).wait_recv()
            chunk(lax.rem(position + nodes - j, nodes))

        loop(1, nodes, arrived)

        def to_cells(index):
            both = jnp.concatenate([work_back[0, index], work_back[1, index]], axis=1)
            both = left_multiply(back_y[...], both)
            value = [both[:, :full_z], both[:, full_z:]]
            if second:
                old = [prior[0, index], prior[1, index]]
                value = [
                    value[0] - (h_a * old[0] - h_i * old[1]),
                    value[1] - (h_b * old[1] + h_i * old[0]),
                ]
            pre[0, index] = value[0]
            pre[1, index] = value[1]

        def stencil(index):
            mid = kappa[index + 1]
            face_after = 0.5 * (mid + kappa[index + 2])
            face_before = 0.5 * (mid + kappa[index])
            face_y = 0.5 * (mid + turn(mid, -1, 0))
            face_z = 0.5 * (mid + turn(mid, -1, 1))
            here = [pre[c, index + 1] for c in range(2)]
            result = []
            for c in range(2):
                total = face_after * (here[c] - pre[c, index + 2])
                total = total + face_before * (here[c] - pre[c, index])
                flux = face_y * (here[c] - turn(here[c], -1, 0))
                total = total + (flux - turn(flux, 1, 0))
                flux = face_z * (here[c] - turn(here[c], -1, 1))
                total = total + (flux - turn(flux, 1, 1))
                result.append(step_length * total)
            result[0] = result[0] + (shift_a * here[0] - shift_i * here[1])
            result[1] = result[1] + (shift_b * here[1] + shift_i * here[0])
            start = [rhs[0, index], rhs[1, index]]
            pairs = [(start[0], result[0]), (start[1], result[1])]
            pairs += [(start[0], result[1]), (start[1], result[0])]
            pairs += [(result[0], result[0]), (result[1], result[1])]
            if second:
                old = [out_one[0, index], out_one[1, index]]
                rest_a = old[0] - (h_a * start[0] - h_i * start[1])
                rest_b = old[1] - (h_b * start[1] + h_i * start[0])
                pairs += [(rest_a, result[0]), (rest_b, result[1])]
                pairs += [(rest_a, result[1]), (rest_b, result[0])]
                pairs += [(rest_a, rest_a), (rest_b, rest_b)]
            else:
                out_one[0, index] = result[0]
                out_one[1, index] = result[1]
                transform_plane(result[0], result[1], forward_y, work.at[pair], index)
                pairs += [(start[0], start[0]), (start[1], start[1])]
            for number, (one, two) in enumerate(pairs):
                dots[number] += folded(one * two)

        dots[...] = jnp.zeros_like(dots)
        ahead = min(3, planes + 2)
        loop(0, ahead, to_cells)

        def both(index):
            stencil(index)
            to_cells(index + ahead)

        loop(0, planes + 2 - ahead, both)
        loop(planes + 2 - ahead, planes, stencil)
        share_dots(phase, 12 if second else 8)

    for pair in range(per_core):
        inner_solve(pair, 2 * pair)
        if pair == 0:
            up.wait_recv()
            down.wait_recv()
            kappa[0] = jnp.where(chip > 0, dif[jnp.maximum(first - 1, 0)], low[...])
            kappa[planes + 1] = jnp.where(
                chip < chips - 1, dif[jnp.minimum(first + planes, slab - 1)], high[...]
            )

            def keep_kappa(index):
                kappa[index + 1] = dif[first + index]

            loop(0, planes, keep_kappa)
        know(pair)
        for part in range(parts):
            exchange(2 * pair, part)
        operate(pair, 2 * pair, False)
        inner_solve(pair, 2 * pair + 1)
        for part in range(parts):
            exchange(2 * pair + 1, part)
        first_sums(pair, 2 * pair)
        operate(pair, 2 * pair + 1, True)

    coefs = []
    for pair in range(per_core):
        loop(1, nodes, lambda j: dots_to(2 * pair + 1, j).wait_recv())
        coefs.append(pair_coefs(sc_all.at[pair], tiles_all.at[2 * pair + 1], nodes))

    def sol_to_core(index):
        return remote(
            sol.at[index], twin_sol.at[index], send_s.at[index], recv_s.at[index], core=twin
        )

    def field_to_chip(j, index):
        peer = lax.rem(chip + j, chips)
        return remote(
            fields.at[peer, index],
            out.at[0, first + index],
            send_f.at[j, index],
            recv_f.at[j, index],
            x=peer,
        )

    def combine(index):
        for i in range(per_core):
            ca, cb = coefs[i]
            one = [pre_all[2 * i, c, index + 1] for c in range(2)]
            two = [pre_all[2 * i + 1, c, index + 1] for c in range(2)]
            sol[index, 2 * i] = ca[0] * one[0] - ca[1] * one[1] + ca[2] * two[0] - ca[3] * two[1]
            sol[index, 2 * i + 1] = (
                cb[0] * one[1] + cb[1] * one[0] + cb[2] * two[1] + cb[3] * two[0]
            )
        sol_to_core(index).start()

    def spread(index):
        sol_to_core(index).wait_recv()

        def field(peer):
            total = None
            for part in range(2 * per_core):
                own = coef_from[peer * cores + core, core * per_core * 2 + part]
                far = coef_from[peer * cores + core, twin * per_core * 2 + part]
                term = own * sol[index, part] + far * twin_sol[index, part]
                total = term if total is None else total + term
            return total

        for j in range(1, chips):
            peer = lax.rem(chip + j, chips)
            fields[peer, index] = field(peer)
            field_to_chip(j, index).start()
        out[0, first + index] = field(chip)

    combine(0)

    def combine_and_spread(index):
        combine(index + 1)
        spread(index)

    loop(0, planes - 1, combine_and_spread)
    spread(planes - 1)

    up.wait_send()
    down.wait_send()
    for share in shares:
        share.wait_send()

    def end(index):
        own_to_core(index).wait_send()
        sol_to_core(index).wait_send()
        for j in range(1, chips):
            to_chip(j, index).wait_send()
            to_core(j, index).wait_send()

    def end_node(j):
        for phase in range(2 * per_core):
            for part in range(parts):
                out_to(phase, part, j).wait_send()
                home_to(phase, part, j).wait_send()
            dots_to(phase, j).wait_send()

    def end_fields(index):
        for j in range(1, chips):
            field_to_chip(j, index).wait_send()
            field_to_chip(j, index).wait_recv()

    loop(0, planes, end)
    loop(1, nodes, end_node)
    loop(0, planes, end_fields)


smem = pl.BlockSpec(memory_space=pltpu.SMEM)
vmem = pl.BlockSpec(memory_space=pltpu.VMEM)
anywhere = pl.BlockSpec(memory_space=pl.ANY)
dma = pltpu.SemaphoreType.DMA


def held(*shape):
    return pltpu.VMEM(shape, jnp.float32)


class Tables:
    def __init__(self, full_x, full_y, full_z, nodes):
        basis_y, basis_z = real_basis(full_y), real_basis(full_z)
        self.y_forward = split_table(basis_y.T, 1, "hlh")
        self.y_back = split_table(basis_y, 1, "hlh")
        self.z_forward = split_table(basis_z, 0, "hhl")
        self.z_back = split_table(basis_z.T, 0, "hhl")
        lam = wave_symbol(full_y)[:, None] + wave_symbol(full_z)[None, :]
        self.lam = lam.astype(np.float32)
        self.nodes = nodes
        waves = wave_symbol(full_x).reshape(full_x // nodes, nodes).T
        self.waves = np.ascontiguousarray(waves).astype(np.float32)
        self.over_nodes = real_basis(nodes).astype(np.float32)


def shards(cores, source, initial, diffusivity):
    chips = lax.axis_size("x")
    steps = chips * cores
    space = lax.axis_size("space")
    nodes = space * chips
    slab, full_y, full_z = diffusivity.shape
    planes = slab // chips
    full_x = slab * space
    rows = full_y // nodes
    tables = Tables(full_x, full_y, full_z, nodes)

    pairs = steps // 2
    per_core = pairs // cores
    geometry = (chips, space, per_core)
    angle = 2.0 * np.pi * np.outer(np.arange(steps), np.arange(pairs)) / steps
    to_pairs = np.stack([np.cos(angle), -np.sin(angle)], axis=2)
    to_pairs[:, 0, 1] = (-1.0) ** np.arange(steps)
    from_pairs = 2.0 * to_pairs / steps
    from_pairs[:, 0] = to_pairs[:, 0] / steps
    decay = (alpha_corner ** (np.arange(steps) / steps))[:, None]
    to_pairs = to_pairs.reshape(steps, steps)
    coef_first = to_pairs[:1].astype(np.float32)
    to_pairs = (to_pairs * decay * step_length).astype(np.float32)
    from_pairs = (from_pairs.reshape(steps, steps) / decay).astype(np.float32)
    root = alpha_corner ** (1.0 / steps)
    base = np.zeros((pairs, 16, full_z), np.float32)
    for pair in range(pairs):
        turned = 2.0 * math.pi * pair / steps
        base[pair, 0] = 1.0 - root * math.cos(turned)
        base[pair, 1] = 1.0 + root if pair == 0 else base[pair, 0]
        base[pair, 2] = root * math.sin(turned)
        base[pair, 4] = 0.0 if pair == 0 else 1.0

    plane = (full_y, full_z)
    phases = 2 * per_core
    parts = 2 if rows % 16 == 0 else 1
    size = rows // parts
    message = (phases, parts, nodes, 4, size, full_z)
    by_part = dma((phases, parts, nodes))
    by_plane, by_node = dma((chips, planes)), dma((phases, nodes))
    return pl.pallas_call(
        functools.partial(window_kernel, geometry),
        out_shape=jax.ShapeDtypeStruct((1, slab, full_y, full_z), jnp.float32),
        in_specs=[smem] * 5 + [vmem] + [anywhere] * 3 + [vmem] * 5,
        out_specs=vmem,
        scratch_shapes=[
            held(planes, *plane),
            held(slab, *plane),
            held(chips, planes, *plane),
            held(chips, planes, *plane),
            held(*plane),
            held(*plane),
            held(8, full_z),
            held(space, 8, full_z),
            held(planes + 2, *plane),
            held(per_core, 16, full_z),
            held(per_core, 2, planes, *plane),
            held(per_core, 2, planes, *plane),
            held(2, planes + 2, *plane),
            held(2, planes - 1, *plane),
            held(2, *plane),
            held(*message),
            held(*message),
            held(*message),
            held(*message),
            held(nodes, 2, size, full_z),
            held(parts, nodes, 3, size, full_z),
            held(phases, 2, planes + 2, *plane),
            held(2, planes, *plane),
            held(12, 8, full_z),
            held(phases, 16, full_z),
            held(phases, nodes, 16, full_z),
            held(planes, phases, *plane),
            held(planes, phases, *plane),
            held(chips, planes, *plane),
            dma((3,)),
            by_plane,
            by_plane,
            by_plane,
            by_plane,
            dma((2,)),
            dma((2,)),
            dma((space,)),
            dma((space,)),
            by_part,
            by_part,
            by_part,
            by_part,
            by_node,
            by_node,
            dma((planes,)),
            dma((planes,)),
            by_plane,
            by_plane,
        ],
        compiler_params=pltpu.CompilerParams(
            vmem_limit_bytes=vmem_bytes, collective_id=0, has_side_effects=True
        ),
        name="window",
    )(
        to_pairs,
        coef_first,
        from_pairs,
        tables.waves,
        tables.over_nodes,
        base,
        source,
        initial,
        diffusivity,
        tables.y_forward,
        tables.z_forward,
        tables.y_back,
        tables.z_back,
        tables.lam,
    )


def solution(mesh):
    cores = 2
    steps = mesh.shape["tm"]
    split = Mesh(
        mesh.devices.reshape(steps // cores, cores, mesh.shape["space"]), ("x", "core", "space")
    )
    in_specs = (P(("x", "core"), "space"), P("space"), P("space"))
    out_specs = P(("x", "core"), "space")
    return jax.shard_map(
        functools.partial(shards, cores),
        mesh=split,
        in_specs=in_specs,
        out_specs=out_specs,
        check_vma=False,
    )
```

```python
import functools
import math

import jax
import jax.numpy as jnp
import ml_dtypes
import numpy as np
from jax import lax
from jax.experimental import pallas as pl
from jax.experimental.pallas import tpu as pltpu
from jax.sharding import Mesh, PartitionSpec as P

alpha_corner = 0.05
step_length = 1.0
vmem_bytes = 56 * 1024 * 1024


def real_basis(length):
    place = np.arange(length)
    angle = 2.0 * np.pi * ((place[:, None] * place[None, :]) % length) / length
    basis = np.where(place[None, :] <= length // 2, np.cos(angle), np.sin(angle))
    return basis / np.sqrt(np.sum(basis * basis, axis=0, keepdims=True))


def wave_symbol(length):
    return 4.0 * np.sin(np.pi * np.arange(length) / length) ** 2


def split_table(table, axis, order):
    high = table.astype(ml_dtypes.bfloat16)
    low = (table - high.astype(np.float64)).astype(ml_dtypes.bfloat16)
    return np.concatenate([high if part == "h" else low for part in order], axis=axis)


def sine_basis(count):
    place = np.arange(1, count + 1)
    return np.sqrt(2.0 / (count + 1)) * np.sin(np.pi * np.outer(place, place) / (count + 1))


def sine_symbol(count):
    return 4.0 * np.sin(np.pi * np.arange(1, count + 1) / (2 * (count + 1))) ** 2


def weighted(factors, values):
    total = None
    for factor, value in zip(factors, values):
        term = float(factor) * value
        total = term if total is None else total + term
    return total


def sine_apply(basis, values):
    count = len(values)
    half = count // 2
    even = [values[j] + values[count - 1 - j] for j in range(half)]
    odd = [values[j] - values[count - 1 - j] for j in range(half)]
    if count % 2:
        even.append(values[half])
    return [
        weighted(basis[k, : len(even)], even) if k % 2 == 0 else weighted(basis[k, :half], odd)
        for k in range(count)
    ]


def halves(values):
    high = values.astype(jnp.bfloat16)
    return high, (values - high.astype(jnp.float32)).astype(jnp.bfloat16)


def left_multiply(table, values):
    high, low = halves(values)
    return jnp.dot(
        table, jnp.concatenate([high, high, low], axis=0), preferred_element_type=jnp.float32
    )


def right_multiply(values, table):
    high, low = halves(values)
    return jnp.dot(
        jnp.concatenate([high, low, high], axis=1), table, preferred_element_type=jnp.float32
    )


def inverse_factors(scalars, symbol):
    shift_a, shift_b, shift_i, mean = scalars[:4]
    diag_a = shift_a + mean * symbol
    diag_b = shift_b + mean * symbol
    scale_a = 1.0 / (diag_a * diag_a + shift_i * shift_i)
    scale_b = 1.0 / (diag_b * diag_b + shift_i * shift_i)
    return diag_a * scale_a, diag_b * scale_b, shift_i * scale_a


def scaled(factors, first, second):
    return (factors[0] * first + factors[2] * second, factors[1] * second - factors[2] * first)


def row(ref, number):
    return ref[pl.ds(number, 1), :]


def transform_plane(first, second, table_y, work, index):
    full_z = first.shape[1]
    both = left_multiply(table_y[...], jnp.concatenate([first, second], axis=1))
    work[0, index] = both[:, :full_z]
    work[1, index] = both[:, full_z:]


def transform_rows(groups, table_z):
    rows = groups[0][0].shape[0]
    stacked = jnp.concatenate([value for group in groups for value in group], axis=0)
    stacked = right_multiply(stacked, table_z[...])
    values = [stacked[n * rows : (n + 1) * rows] for n in range(stacked.shape[0] // rows)]
    size = len(groups[0])
    return [values[c * size : (c + 1) * size] for c in range(len(groups))]


def loop(start, stop, body):
    def step(index, carry):
        body(index)
        return carry

    lax.fori_loop(start, stop, step, 0)


def remote(src, dst, send, recv, **where):
    return pltpu.make_async_remote_copy(
        src_ref=src,
        dst_ref=dst,
        send_sem=send,
        recv_sem=recv,
        device_id=where,
        device_id_type=pl.DeviceIdType.MESH,
    )


def greet(barrier, **where):
    pl.semaphore_signal(
        barrier, inc=1, device_id=where, device_id_type=pl.DeviceIdType.MESH
    )


def node_place(node, chips):
    return {"space": lax.div(node, chips), "x": lax.rem(node, chips)}


def dot_rows(tiles, nodes, count):
    total = tiles[0]
    for node in range(1, nodes):
        total = total + tiles[node]
    total = jnp.sum(total, axis=1, keepdims=True)
    return [
        jnp.broadcast_to(total[number : number + 1], (1, tiles.shape[2]))
        for number in range(count)
    ]


def pair_coefs(sc, tiles, nodes):
    sums = dot_rows(tiles, nodes, 12)
    mixed = row(sc, 4)
    h_i = row(sc, 7)
    top = hermitian(mixed, sums[0], sums[1], sums[2], sums[3])
    length = hermitian(mixed, sums[4], sums[5], sums[4], sums[4])
    diag = hermitian(mixed, sums[6], sums[7], sums[8], sums[9])
    left = hermitian(mixed, sums[10], sums[11], sums[10], sums[10])
    coefs = []
    for which in range(2):
        h_r, norm2, left2 = row(sc, 5 + which), row(sc, 8 + which), left[which]
        root = jnp.sqrt(norm2) * jnp.sqrt(left2)
        c1, c2 = small_solve(
            norm2,
            (h_r, h_i),
            left2 / norm2,
            [part / root for part in (top[which], top[2])],
            [part / left2 for part in (diag[which], diag[2])],
            length[which] / left2,
        )
        scale_one, scale_two = 1.0 / jnp.sqrt(norm2), 1.0 / jnp.sqrt(left2)
        coefs.append((c1[0] * scale_one, c1[1] * scale_one, c2[0] * scale_two, c2[1] * scale_two))
    return coefs


def turn(values, amount, axis):
    return pltpu.roll(values, amount % values.shape[axis], axis)


def folded(values):
    return jnp.sum(values.reshape(-1, 8, values.shape[-1]), axis=0)


def hermitian(mixed, d00, d11, d01, d10):
    return d00 + mixed * d11, d11 + mixed * d00, mixed * (d01 - d10)


def small_solve(norm2, h11, h21_2, h12, h22, gram_second):
    gram_first = h11[0] * h11[0] + h11[1] * h11[1] + h21_2
    sub = jnp.sqrt(h21_2)
    cross_real = h11[0] * h12[0] + h11[1] * h12[1] + sub * h22[0]
    cross_imag = h11[0] * h12[1] - h11[1] * h12[0] + sub * h22[1]
    norm = jnp.sqrt(norm2)
    one = (norm * h11[0], -norm * h11[1])
    two = (norm * h12[0], -norm * h12[1])
    det = gram_first * gram_second - (cross_real * cross_real + cross_imag * cross_imag)
    c1 = (
        (gram_second * one[0] - (cross_real * two[0] - cross_imag * two[1])) / det,
        (gram_second * one[1] - (cross_real * two[1] + cross_imag * two[0])) / det,
    )
    c2 = (
        (gram_first * two[0] - (cross_real * one[0] + cross_imag * one[1])) / det,
        (gram_first * two[1] - (cross_real * one[1] - cross_imag * one[0])) / det,
    )
    return c1, c2


def window_kernel(
    geometry,
    coef_to,
    coef_first,
    coef_from,
    waves,
    table,
    base,
    source,
    initial,
    diffusivity,
    forward_y,
    forward_z,
    back_y,
    back_z,
    lam,
    out,
    *scratch,
):
    chips, space, per_core = geometry
    (
        opening, dif, mine, other, low, high, share_tile, share_tiles, kappa, sc_all, rhs_all,
        work, work_back, inner, edge, sent_all, got_all, back_all, res_all, spec, known,
        pre_all, out_one, dots, tile_all, tiles_all, sol, twin_sol, fields,
    ) = scratch[:29]
    (
        local, send_x, recv_x, send_c, recv_c, send_h, recv_h, send_m, recv_m,
        send_o, recv_o, send_b, recv_b, send_t, recv_t, send_s, recv_s, send_f, recv_f,
    ) = scratch[29:]
    cores = 2
    nodes = space * chips
    slab, full_y, full_z = dif.shape
    planes = slab // chips
    count = planes - 1
    rows = full_y // nodes
    per_node = waves.shape[1]
    parts, size = sent_all.shape[1], sent_all.shape[4]
    basis, symbol = sine_basis(count), sine_symbol(count)
    chip, core, place = lax.axis_index("x"), lax.axis_index("core"), lax.axis_index("space")
    twin = cores - 1 - core
    position = place * chips + chip
    first = chip * planes

    near = max(1, nodes // 4)

    def far_first(body):
        loop(near, nodes, body)
        loop(1, near, body)

    def node_at(j):
        return lax.rem(position + j, nodes)

    loads = [
        pltpu.make_async_copy(diffusivity, dif, local.at[0]),
        pltpu.make_async_copy(initial.at[pl.ds(first, planes)], opening, local.at[1]),
        pltpu.make_async_copy(source.at[0, pl.ds(first, planes)], mine.at[chip], local.at[2]),
    ]
    for load in loads:
        load.start()

    barrier = pltpu.get_barrier_semaphore()
    loop(1, nodes, lambda j: greet(barrier, **node_place(node_at(j), chips)))
    greet(barrier, core=twin)
    pl.semaphore_wait(barrier, nodes)

    def to_chip(j, index):
        peer = lax.rem(chip + j, chips)
        return remote(
            source.at[0, peer * planes + index],
            mine.at[chip, index],
            send_x.at[j, index],
            recv_x.at[j, index],
            x=peer,
        )

    def own_to_core(index):
        return remote(
            source.at[0, first + index],
            other.at[chip, index],
            send_c.at[0, index],
            recv_c.at[0, index],
            core=twin,
        )

    def to_core(j, index):
        sender = lax.rem(chip + chips - j, chips)
        return remote(
            mine.at[sender, index],
            other.at[sender, index],
            send_c.at[j, index],
            recv_c.at[j, index],
            core=twin,
        )

    def begin(index):
        for j in range(1, chips):
            to_chip(j, index).start()

    loop(0, planes, begin)
    loop(0, planes, lambda index: own_to_core(index).start())
    loads[0].wait()
    after, before = lax.rem(place + 1, space), lax.rem(place + space - 1, space)
    up = remote(dif.at[slab - 1], low, send_h.at[0], recv_h.at[0], space=after)
    down = remote(dif.at[0], high, send_h.at[1], recv_h.at[1], space=before)
    up.start()
    down.start()
    share_tile[...] = jnp.zeros_like(share_tile)

    def add_plane(index):
        share_tile[...] += folded(dif[index])

    loop(0, slab, add_plane)
    shares = [
        remote(
            share_tile,
            share_tiles.at[place],
            send_m.at[j],
            recv_m.at[j],
            space=lax.rem(place + j, space),
        )
        for j in range(1, space)
    ]
    for share in shares:
        share.start()
    share_tiles[place] = share_tile[...]
    loads[1].wait()
    loads[2].wait()

    def relay(index):
        for j in range(1, chips):
            to_chip(j, index).wait_recv()
            to_core(j, index).start()

    def process(index):
        own_to_core(index).wait_recv()
        for j in range(1, chips):
            to_core(j, index).wait_recv()
        for i in range(per_core):
            values = []
            for c in range(2):
                column = (core * per_core + i) * 2 + c
                total = coef_first[0, column] * opening[index]
                for n in range(chips):
                    total = total + coef_to[n * cores + core, column] * mine[n, index]
                    total = total + coef_to[n * cores + twin, column] * other[n, index]
                rhs_all[i, c, index] = total
                values.append(total)
            transform_plane(values[0], values[1], forward_y, work.at[i], index)

    relay(0)

    def relay_and_process(index):
        relay(index + 1)
        process(index)

    loop(0, planes - 1, relay_and_process)
    process(planes - 1)

    for share in shares:
        share.wait_recv()
    total = share_tiles[0]
    for j in range(1, space):
        total = total + share_tiles[j]
    total = jnp.sum(jnp.sum(total, axis=0, keepdims=True), axis=1, keepdims=True)
    cells = slab * space * full_y * full_z
    for i in range(per_core):
        sc_all[i] = base[core * per_core + i]
        sc_all[i, pl.ds(3, 1)] = jnp.broadcast_to(total / cells, (1, full_z))

    def out_to(phase, part, j):
        peer = node_at(j)
        return remote(
            sent_all.at[phase, part, peer],
            got_all.at[phase, part, position],
            send_o.at[phase, part, j],
            recv_o.at[phase, part, j],
            **node_place(peer, chips),
        )

    def home_to(phase, part, j):
        peer = node_at(j)
        return remote(
            back_all.at[phase, part, peer],
            res_all.at[phase, part, position],
            send_b.at[phase, part, j],
            recv_b.at[phase, part, j],
            **node_place(peer, chips),
        )

    def dots_to(phase, j):
        return remote(
            tile_all.at[phase],
            tiles_all.at[phase, position],
            send_t.at[phase, j],
            recv_t.at[phase, j],
            **node_place(node_at(j), chips),
        )

    def share_dots(phase, number_of):
        tile = tile_all.at[phase]
        tile[...] = jnp.zeros(tile.shape, jnp.float32)
        for number in range(number_of):
            tile[pl.ds(number, 1), :] = jnp.sum(dots[number], axis=0, keepdims=True)
        loop(1, nodes, lambda j: dots_to(phase, j).start())
        tiles_all[phase, position] = tile[...]

    def inner_solve(pair, phase):
        sc, spectrum = sc_all.at[pair], work.at[pair]
        sent = sent_all.at[phase]
        scalars = [row(sc, number) for number in range(4)]
        mean = scalars[3]

        def chunk(index):
            rng = pl.ds(pl.multiple_of(index * rows, rows), rows)
            spectral = transform_rows(
                [[spectrum[c, j, rng] for j in range(planes)] for c in range(2)], forward_z
            )
            values = [sine_apply(basis, spectral[c][:count]) for c in range(2)]
            ends = [[None, None], [None, None]]
            for k in range(count):
                factors = inverse_factors(scalars, lam[rng] + float(symbol[k]))
                for c, value in enumerate(scaled(factors, values[0][k], values[1][k])):
                    inner[c, k, rng] = value
                    for end, at in ((0, 0), (1, count - 1)):
                        term = float(basis[at, k]) * value
                        ends[c][end] = term if k == 0 else ends[c][end] + term
            for c in range(2):
                own = spectral[c][count]
                edge[c, rng] = own
                for number, value in ((c, own + mean * ends[c][1]), (2 + c, mean * ends[c][0])):
                    for part in range(parts):
                        sent[part, index, number] = value[part * size : (part + 1) * size]

        def send(j):
            chunk(node_at(j))
            out_to(phase, 0, j).start()

        far_first(send)
        for part in range(1, parts):
            far_first(lambda j: out_to(phase, part, j).start())
        chunk(position)

    def know(pair):
        scalars = [row(sc_all.at[pair], number) for number in range(4)]
        lam_value = lam[pl.ds(pl.multiple_of(position * rows, rows), rows)]

        def one(mode):
            factors = None
            for part in range(per_node):
                term = inverse_factors(scalars, lam_value + waves[mode, part])
                factors = term if factors is None else [a + b for a, b in zip(factors, term)]
            for number in range(3):
                value = factors[number] * (1.0 / per_node)
                for part in range(parts):
                    known[part, mode, number] = value[part * size : (part + 1) * size]

        loop(0, nodes, one)

    def exchange(phase, part):
        got, back = got_all.at[phase, part], back_all.at[phase, part]
        got[position] = sent_all[phase, part, position]
        loop(1, nodes, lambda j: out_to(phase, part, j).wait_recv())

        def to_modes(mode):
            values = []
            for c in range(2):
                total = None
                for d in range(nodes):
                    term = table[d, mode] * (got[d, c] + got[(d + 1) % nodes, 2 + c])
                    total = term if total is None else total + term
                values.append(total)
            factors = [known[part, mode, number] for number in range(3)]
            spec[mode, 0], spec[mode, 1] = scaled(factors, values[0], values[1])

        loop(0, nodes, to_modes)

        def from_modes(j):
            node = node_at(j)
            following = node_at(j + 1)
            for c in range(2):
                total = None
                for mode in range(nodes):
                    term = table[node, mode] * spec[mode, c]
                    total = term if total is None else total + term
                back[node, c] = total
                back[following, 2 + c] = total

        def send_home(j):
            from_modes(j)
            home_to(phase, part, j).start()

        from_modes(near - 1)
        loop(near, nodes, send_home)
        if near > 1:
            from_modes(0)
            loop(1, near - 1, send_home)
            home_to(phase, part, near - 1).start()
        res_all[phase, part, position] = back[position]

    def first_sums(pair, phase):
        sc = sc_all.at[pair]
        loop(1, nodes, lambda j: dots_to(phase, j).wait_recv())
        sums = dot_rows(tiles_all.at[phase], nodes, 8)
        mixed = row(sc, 4)
        norm_a, norm_b, _ = hermitian(mixed, sums[6], sums[7], sums[6], sums[6])
        top = hermitian(mixed, sums[0], sums[1], sums[2], sums[3])
        values = (top[0] / norm_a, top[1] / norm_b, top[2] / norm_a, norm_a, norm_b)
        for number, value in enumerate(values):
            sc[pl.ds(5 + number, 1), :] = value

    def operate(pair, phase, second):
        sc, res, rhs = sc_all.at[pair], res_all.at[phase], rhs_all.at[pair]
        pre = pre_all.at[phase]
        prior = pre_all.at[2 * pair]
        scalars = [row(sc, number) for number in range(4)]
        shift_a, shift_b, shift_i, mean = scalars
        if second:
            h_a, h_b, h_i = [row(sc, number) for number in range(5, 8)]

        def chunk(index):
            rng = pl.ds(pl.multiple_of(index * rows, rows), rows)
            ends = [
                jnp.concatenate([res[part, index, number] for part in range(parts)], axis=0)
                for number in range(4)
            ]
            own, left = ends[:2], ends[2:]
            lam_value = lam[rng]
            values = [[], []]
            for k in range(count):
                factors = inverse_factors(scalars, lam_value + float(symbol[k]))
                ends = [
                    mean * (float(basis[0, k]) * left[c] + float(basis[count - 1, k]) * own[c])
                    for c in range(2)
                ]
                for c, value in enumerate(scaled(factors, ends[0], ends[1])):
                    values[c].append(inner[c, k, rng] + value)
            diag = mean * (lam_value + 2.0)
            lifted = (
                (shift_a + diag) * own[0] - shift_i * own[1],
                (shift_b + diag) * own[1] + shift_i * own[0],
            )
            lines = []
            for c in range(2):
                solved = sine_apply(basis, values[c])
                beyond = (lifted[c] - edge[c, rng]) / mean - solved[-1]
                lines.append([left[c], *solved, own[c], beyond])
            for c, line in enumerate(transform_rows(lines, back_z)):
                for j, value in enumerate(line):
                    work_back[c, j, rng] = value

        chunk(position)

        def arrived(j):
            for part in range(parts):
                home_to(phase, part, j).wait_recv()
            chunk(lax.rem(position + nodes - j, nodes))

        far_first(arrived)

        def to_cells(index):
            both = jnp.concatenate([work_back[0, index], work_back[1, index]], axis=1)
            both = left_multiply(back_y[...], both)
            value = [both[:, :full_z], both[:, full_z:]]
            if second:
                old = [prior[0, index], prior[1, index]]
                value = [
                    value[0] - (h_a * old[0] - h_i * old[1]),
                    value[1] - (h_b * old[1] + h_i * old[0]),
                ]
            pre[0, index] = value[0]
            pre[1, index] = value[1]

        def stencil(index):
            mid = kappa[index + 1]
            face_after = 0.5 * (mid + kappa[index + 2])
            face_before = 0.5 * (mid + kappa[index])
            face_y = 0.5 * (mid + turn(mid, -1, 0))
            face_z = 0.5 * (mid + turn(mid, -1, 1))
            here = [pre[c, index + 1] for c in range(2)]
            result = []
            for c in range(2):
                total = face_after * (here[c] - pre[c, index + 2])
                total = total + face_before * (here[c] - pre[c, index])
                flux = face_y * (here[c] - turn(here[c], -1, 0))
                total = total + (flux - turn(flux, 1, 0))
                flux = face_z * (here[c] - turn(here[c], -1, 1))
                total = total + (flux - turn(flux, 1, 1))
                result.append(step_length * total)
            result[0] = result[0] + (shift_a * here[0] - shift_i * here[1])
            result[1] = result[1] + (shift_b * here[1] + shift_i * here[0])
            start = [rhs[0, index], rhs[1, index]]
            pairs = [(start[0], result[0]), (start[1], result[1])]
            pairs += [(start[0], result[1]), (start[1], result[0])]
            pairs += [(result[0], result[0]), (result[1], result[1])]
            if second:
                old = [out_one[0, index], out_one[1, index]]
                rest_a = old[0] - (h_a * start[0] - h_i * start[1])
                rest_b = old[1] - (h_b * start[1] + h_i * start[0])
                pairs += [(rest_a, result[0]), (rest_b, result[1])]
                pairs += [(rest_a, result[1]), (rest_b, result[0])]
                pairs += [(rest_a, rest_a), (rest_b, rest_b)]
            else:
                out_one[0, index] = result[0]
                out_one[1, index] = result[1]
                transform_plane(result[0], result[1], forward_y, work.at[pair], index)
                pairs += [(start[0], start[0]), (start[1], start[1])]
            for number, (one, two) in enumerate(pairs):
                dots[number] += folded(one * two)

        dots[...] = jnp.zeros_like(dots)
        ahead = min(3, planes + 2)
        loop(0, ahead, to_cells)

        def both(index):
            stencil(index)
            to_cells(index + ahead)

        loop(0, planes + 2 - ahead, both)
        loop(planes + 2 - ahead, planes, stencil)
        share_dots(phase, 12 if second else 8)

    for pair in range(per_core):
        inner_solve(pair, 2 * pair)
        if pair == 0:
            up.wait_recv()
            down.wait_recv()
            kappa[0] = jnp.where(chip > 0, dif[jnp.maximum(first - 1, 0)], low[...])
            kappa[planes + 1] = jnp.where(
                chip < chips - 1, dif[jnp.minimum(first + planes, slab - 1)], high[...]
            )

            def keep_kappa(index):
                kappa[index + 1] = dif[first + index]

            loop(0, planes, keep_kappa)
        know(pair)
        for part in range(parts):
            exchange(2 * pair, part)
        operate(pair, 2 * pair, False)
        inner_solve(pair, 2 * pair + 1)
        for part in range(parts):
            exchange(2 * pair + 1, part)
        first_sums(pair, 2 * pair)
        operate(pair, 2 * pair + 1, True)

    coefs = []
    for pair in range(per_core):
        loop(1, nodes, lambda j: dots_to(2 * pair + 1, j).wait_recv())
        coefs.append(pair_coefs(sc_all.at[pair], tiles_all.at[2 * pair + 1], nodes))

    def sol_to_core(index):
        return remote(
            sol.at[index], twin_sol.at[index], send_s.at[index], recv_s.at[index], core=twin
        )

    def field_to_chip(j, index):
        peer = lax.rem(chip + j, chips)
        return remote(
            fields.at[peer, index],
            out.at[0, first + index],
            send_f.at[j, index],
            recv_f.at[j, index],
            x=peer,
        )

    def combine(index):
        for i in range(per_core):
            ca, cb = coefs[i]
            one = [pre_all[2 * i, c, index + 1] for c in range(2)]
            two = [pre_all[2 * i + 1, c, index + 1] for c in range(2)]
            sol[index, 2 * i] = ca[0] * one[0] - ca[1] * one[1] + ca[2] * two[0] - ca[3] * two[1]
            sol[index, 2 * i + 1] = (
                cb[0] * one[1] + cb[1] * one[0] + cb[2] * two[1] + cb[3] * two[0]
            )
        sol_to_core(index).start()

    def spread(index):
        sol_to_core(index).wait_recv()

        def field(peer):
            total = None
            for part in range(2 * per_core):
                own = coef_from[peer * cores + core, core * per_core * 2 + part]
                far = coef_from[peer * cores + core, twin * per_core * 2 + part]
                term = own * sol[index, part] + far * twin_sol[index, part]
                total = term if total is None else total + term
            return total

        for j in range(1, chips):
            peer = lax.rem(chip + j, chips)
            fields[peer, index] = field(peer)
            field_to_chip(j, index).start()
        out[0, first + index] = field(chip)

    combine(0)

    def combine_and_spread(index):
        combine(index + 1)
        spread(index)

    loop(0, planes - 1, combine_and_spread)
    spread(planes - 1)

    up.wait_send()
    down.wait_send()
    for share in shares:
        share.wait_send()

    def end(index):
        own_to_core(index).wait_send()
        sol_to_core(index).wait_send()
        for j in range(1, chips):
            to_chip(j, index).wait_send()
            to_core(j, index).wait_send()

    def end_node(j):
        for phase in range(2 * per_core):
            for part in range(parts):
                out_to(phase, part, j).wait_send()
                home_to(phase, part, j).wait_send()
            dots_to(phase, j).wait_send()

    def end_fields(index):
        for j in range(1, chips):
            field_to_chip(j, index).wait_send()
            field_to_chip(j, index).wait_recv()

    loop(0, planes, end)
    loop(1, nodes, end_node)
    loop(0, planes, end_fields)


def place_kernel(result, out):
    out[...] = result[...]


smem = pl.BlockSpec(memory_space=pltpu.SMEM)
vmem = pl.BlockSpec(memory_space=pltpu.VMEM)
anywhere = pl.BlockSpec(memory_space=pl.ANY)
dma = pltpu.SemaphoreType.DMA


def held(*shape):
    return pltpu.VMEM(shape, jnp.float32)


class Tables:
    def __init__(self, full_x, full_y, full_z, nodes):
        basis_y, basis_z = real_basis(full_y), real_basis(full_z)
        self.y_forward = split_table(basis_y.T, 1, "hlh")
        self.y_back = split_table(basis_y, 1, "hlh")
        self.z_forward = split_table(basis_z, 0, "hhl")
        self.z_back = split_table(basis_z.T, 0, "hhl")
        lam = wave_symbol(full_y)[:, None] + wave_symbol(full_z)[None, :]
        self.lam = lam.astype(np.float32)
        self.nodes = nodes
        waves = wave_symbol(full_x).reshape(full_x // nodes, nodes).T
        self.waves = np.ascontiguousarray(waves).astype(np.float32)
        self.over_nodes = real_basis(nodes).astype(np.float32)


def shards(cores, source, initial, diffusivity):
    chips = lax.axis_size("x")
    steps = chips * cores
    space = lax.axis_size("space")
    nodes = space * chips
    slab, full_y, full_z = diffusivity.shape
    planes = slab // chips
    full_x = slab * space
    rows = full_y // nodes
    tables = Tables(full_x, full_y, full_z, nodes)

    pairs = steps // 2
    per_core = pairs // cores
    geometry = (chips, space, per_core)
    angle = 2.0 * np.pi * np.outer(np.arange(steps), np.arange(pairs)) / steps
    to_pairs = np.stack([np.cos(angle), -np.sin(angle)], axis=2)
    to_pairs[:, 0, 1] = (-1.0) ** np.arange(steps)
    from_pairs = 2.0 * to_pairs / steps
    from_pairs[:, 0] = to_pairs[:, 0] / steps
    decay = (alpha_corner ** (np.arange(steps) / steps))[:, None]
    to_pairs = to_pairs.reshape(steps, steps)
    coef_first = to_pairs[:1].astype(np.float32)
    to_pairs = (to_pairs * decay * step_length).astype(np.float32)
    from_pairs = (from_pairs.reshape(steps, steps) / decay).astype(np.float32)
    root = alpha_corner ** (1.0 / steps)
    base = np.zeros((pairs, 16, full_z), np.float32)
    for pair in range(pairs):
        turned = 2.0 * math.pi * pair / steps
        base[pair, 0] = 1.0 - root * math.cos(turned)
        base[pair, 1] = 1.0 + root if pair == 0 else base[pair, 0]
        base[pair, 2] = root * math.sin(turned)
        base[pair, 4] = 0.0 if pair == 0 else 1.0

    plane = (full_y, full_z)
    phases = 2 * per_core
    parts = 2 if rows % 16 == 0 else 1
    size = rows // parts
    message = (phases, parts, nodes, 4, size, full_z)
    by_part = dma((phases, parts, nodes))
    by_plane, by_node = dma((chips, planes)), dma((phases, nodes))
    result = pl.pallas_call(
        functools.partial(window_kernel, geometry),
        out_shape=jax.ShapeDtypeStruct((1, slab, full_y, full_z), jnp.float32),
        in_specs=[smem] * 5 + [vmem] + [anywhere] * 3 + [vmem] * 5,
        out_specs=vmem,
        scratch_shapes=[
            held(planes, *plane),
            held(slab, *plane),
            held(chips, planes, *plane),
            held(chips, planes, *plane),
            held(*plane),
            held(*plane),
            held(8, full_z),
            held(space, 8, full_z),
            held(planes + 2, *plane),
            held(per_core, 16, full_z),
            held(per_core, 2, planes, *plane),
            held(per_core, 2, planes, *plane),
            held(2, planes + 2, *plane),
            held(2, planes - 1, *plane),
            held(2, *plane),
            held(*message),
            held(*message),
            held(*message),
            held(*message),
            held(nodes, 2, size, full_z),
            held(parts, nodes, 3, size, full_z),
            held(phases, 2, planes + 2, *plane),
            held(2, planes, *plane),
            held(12, 8, full_z),
            held(phases, 16, full_z),
            held(phases, nodes, 16, full_z),
            held(planes, phases, *plane),
            held(planes, phases, *plane),
            held(chips, planes, *plane),
            dma((3,)),
            by_plane,
            by_plane,
            by_plane,
            by_plane,
            dma((2,)),
            dma((2,)),
            dma((space,)),
            dma((space,)),
            by_part,
            by_part,
            by_part,
            by_part,
            by_node,
            by_node,
            dma((planes,)),
            dma((planes,)),
            by_plane,
            by_plane,
        ],
        compiler_params=pltpu.CompilerParams(
            vmem_limit_bytes=vmem_bytes, collective_id=0, has_side_effects=True
        ),
        name="window",
    )(
        to_pairs,
        coef_first,
        from_pairs,
        tables.waves,
        tables.over_nodes,
        base,
        source,
        initial,
        diffusivity,
        tables.y_forward,
        tables.z_forward,
        tables.y_back,
        tables.z_back,
        tables.lam,
    )
    block = pl.BlockSpec((1, max(1, slab // 8), full_y, full_z), lambda index: (0, index, 0, 0))
    return pl.pallas_call(
        place_kernel,
        grid=(slab // block.block_shape[1],),
        out_shape=jax.ShapeDtypeStruct(result.shape, jnp.float32),
        in_specs=[block],
        out_specs=block,
        compiler_params=pltpu.CompilerParams(vmem_limit_bytes=vmem_bytes),
        name="place",
    )(result)


def solution(mesh):
    cores = 2
    steps = mesh.shape["tm"]
    split = Mesh(
        mesh.devices.reshape(steps // cores, cores, mesh.shape["space"]), ("x", "core", "space")
    )
    in_specs = (P(("x", "core"), "space"), P("space"), P("space"))
    out_specs = P(("x", "core"), "space")
    return jax.shard_map(
        functools.partial(shards, cores),
        mesh=split,
        in_specs=in_specs,
        out_specs=out_specs,
        check_vma=False,
    )
```
